256 devices in a mesh: section: 2 (over y_hi), ctx: 16 (over z, core), head: 8 (over x, y_lo).
Axes of the slice: x: 4, y: 4 (y_hi: 2, y_lo: 2; y = y_hi * 2 + y_lo), z: 8, core: 2. Of those that a mesh axis runs over, the one named last changes fastest.
Arguments:
- queries: bfloat16 [2, 4096, 6144], P('section', ('ctx', 'head'))
- noisy_keys: bfloat16 [2, 4096, 1024], P('section', ('ctx', 'head'))
- noisy_values: bfloat16 [2, 4096, 1024], P('section', ('ctx', 'head')), may hold values from -6 to 6
- clean_keys: bfloat16 [2, 4096, 1024], P('section', ('ctx', 'head')), may hold values from -6 to 6
- clean_values: bfloat16 [2, 4096, 1024], P('section', ('ctx', 'head')), may hold values from -6 to 6
- clip_order: int32 [2], replicated, may hold values from 0 to 1, each once
- key_counts: int32 [2, 32], replicated, may hold values from 2 to 128, as said below
- tile_mask: int32 [2, 32, 32], replicated, may hold values from 0 to 1, as said below
Outputs:
- attended: bfloat16 [2, 4096, 6144], P('section', ('ctx', 'head'))
The draws below stay inside these ranges and needn't reach their ends.
Inputs may be any that keep to these rules, and one draw needn't show every extreme that they name: `clip_order`: the two sections hold different clips; the smaller number is the earlier clip. The tiles of a clip fall into consecutive frame groups of one or more tiles, with two groups or more; key_counts is 128 in every tile but the last of a group, and 2 to 128 in the last tile of a group (padding at its end); the valid tokens of a tile come first in it; some tile holds 128 valid tokens and some holds 2. With the frame groups of key_counts numbered in order, tile_mask[s, i, j] = 1 exactly when the group of tile j is not later than the group of tile i.
All inputs are finite; a program needn't handle non-finite values.
Results may differ from the reference program's by a relative error of at most 0.007.
Values may be sent and summed in bfloat16 or wider, within the bound.
A program may use at most 64 MiB of HBM per device.

```python
import jax
import jax.numpy as jnp
from jax import lax

HEADS = 48
KV_HEADS = 8
HD = 128
TILE = 128
GROUP = 4096


def shared_normal(key):
    return jax.random.normal(jax.random.fold_in(key, 11), (2, GROUP, KV_HEADS * HD), jnp.float32)


def tile_layout(key):
    base = jax.random.fold_in(key, 51)
    tile_total = GROUP // TILE
    tile_ids = jnp.arange(tile_total, dtype=jnp.int32)
    flags = jax.random.randint(jax.random.fold_in(base, 1), (2, tile_total), 0, 2)
    flags = jnp.where(tile_ids[None, :] == tile_total - 1, 1, flags)
    flags = jnp.where(tile_ids[None, :] == tile_total // 2 - 1, 1, flags)
    flags = jnp.where(tile_ids[None, :] == 0, 0, flags)
    block_ids = jnp.cumsum(flags, axis=1) - flags
    lengths = jax.random.randint(jax.random.fold_in(base, 2), (2, tile_total), 2, TILE + 1)
    return (flags, block_ids, lengths)


def draw_noisy_keys(key, part):
    common = shared_normal(key)
    return jnp.clip(common, -6.0, 6.0).astype(jnp.bfloat16)


def draw_queries(key, part):
    key = jax.random.fold_in(key, 21)
    values_out = jax.random.normal(jax.random.fold_in(key, 1), (2, GROUP, HEADS * HD), jnp.float32)
    return jnp.clip(values_out, -128.0, 128.0).astype(jnp.bfloat16)


def draw_key_counts(key, part):
    flags, block_ids, lengths = tile_layout(key)
    tile_total = GROUP // TILE
    tile_ids = jnp.arange(tile_total, dtype=jnp.int32)
    counts = jnp.where(flags == 1, lengths, TILE)
    counts = jnp.where(tile_ids[None, :] == tile_total // 2 - 1, 2, counts)
    return counts.astype(jnp.int32)


def draw_tile_mask(key, part):
    flags, block_ids, lengths = tile_layout(key)
    seen = block_ids[:, None, :] <= block_ids[:, :, None]
    return seen.astype(jnp.int32)


def block_scale(stream_key, shape, cuts, smallest, high):
    def one(axis_at, parts):
        steps = jax.random.uniform(jax.random.fold_in(jax.random.fold_in(stream_key, 6), axis_at), (parts,), jnp.float32, smallest / len(cuts), high / len(cuts))
        return jnp.repeat(jnp.exp(steps), shape[axis_at] // parts).reshape((-1,) + (1,) * (len(shape) - axis_at - 1))

    factor_of = one(*cuts[0])
    for cut in cuts[1:]:
        factor_of = factor_of * one(*cut)
    return factor_of


def normal_values(own_key, dims, width, most, pieces=(), kind=jnp.bfloat16):
    array = width * jax.random.normal(own_key, dims, jnp.float32)
    if pieces:
        array = array * block_scale(own_key, dims, pieces, -0.22, 0.18)
    return jnp.clip(array, -most, most).astype(kind)


def setup_inputs(seed: int = 0) -> dict:
    keys = jax.random.split(jax.random.key(seed), 9)
    return {
        "queries": draw_queries(jax.random.fold_in(keys[8], 71), 0),
        "noisy_keys": draw_noisy_keys(jax.random.fold_in(keys[8], 71), 0),
        "noisy_values": normal_values(keys[2], (2, GROUP, KV_HEADS * HD), 1.0, 6.0, ((0, 2), (1, 128))),
        "clean_keys": normal_values(keys[3], (2, GROUP, KV_HEADS * HD), 1.0, 6.0, ((0, 2), (1, 128))),
        "clean_values": normal_values(keys[4], (2, GROUP, KV_HEADS * HD), 1.0, 6.0, ((0, 2), (1, 128))),
        "clip_order": jax.random.permutation(keys[5], 2).astype(jnp.int32),
        "key_counts": draw_key_counts(jax.random.fold_in(keys[8], 71), 0),
        "tile_mask": draw_tile_mask(jax.random.fold_in(keys[8], 71), 0),
    }


NEG_FILL = -1.0e30


def reference(queries, noisy_keys, noisy_values, clean_keys, clean_values, clip_order, key_counts, tile_mask):
    score_scale = HD ** -0.5
    group_size = HEADS // KV_HEADS
    positions = jnp.arange(GROUP, dtype=jnp.int32)
    tile_of = positions // TILE
    within = positions % TILE
    results = []
    for section_number in range(2):
        other_section = 1 - section_number
        own_open = (tile_mask[section_number][tile_of][:, tile_of] > 0) & (within < key_counts[section_number][tile_of])[None, :]
        earlier = clip_order[other_section] < clip_order[section_number]
        clean_open = jnp.broadcast_to(((within < key_counts[other_section][tile_of]) & earlier)[None, :], (GROUP, GROUP))
        allowed = jnp.concatenate([clean_open, own_open], axis=1)
        key_all = jnp.concatenate([clean_keys[other_section], noisy_keys[section_number]], axis=0).reshape(2 * GROUP, KV_HEADS, HD)
        value_all = jnp.concatenate([clean_values[other_section], noisy_values[section_number]], axis=0).reshape(2 * GROUP, KV_HEADS, HD)
        query_all = queries[section_number].reshape(GROUP, HEADS, HD)

        def one_head(head_number):
            group_number = head_number // group_size
            query_rows = lax.dynamic_index_in_dim(query_all, head_number, 1, keepdims=False)
            key_rows = lax.dynamic_index_in_dim(key_all, group_number, 1, keepdims=False)
            value_rows = lax.dynamic_index_in_dim(value_all, group_number, 1, keepdims=False)
            scores = jnp.dot(query_rows, key_rows.T, preferred_element_type=jnp.float32) * score_scale
            scores = jnp.where(allowed, scores, NEG_FILL)
            row_top = jnp.max(scores, axis=1, keepdims=True)
            weights = jnp.where(allowed, jnp.exp(scores - row_top), 0.0)
            row_total = jnp.sum(weights, axis=1, keepdims=True)
            mixture = jnp.dot(weights.astype(jnp.bfloat16), value_rows, preferred_element_type=jnp.float32)
            return mixture / row_total

        per_head = lax.map(one_head, jnp.arange(HEADS, dtype=jnp.int32))
        results.append(jnp.transpose(per_head, (1, 0, 2)).reshape(GROUP, HEADS * HD).astype(jnp.bfloat16))
    return jnp.stack(results)
```

```python
import functools
import math

import jax
import jax.numpy as jnp
from jax import lax
from jax.experimental import pallas as pl
from jax.experimental.pallas import tpu as pltpu
from jax.sharding import PartitionSpec as P

MESH = pl.DeviceIdType.MESH
HD = 128
TILE = 128
CLOSED = -1e30
EXP_SCALE = math.log2(math.e) * HD ** -0.5


def remote(src, dst, send_sem, recv_sem, device):
    return pltpu.make_async_remote_copy(
        src_ref=src,
        dst_ref=dst,
        send_sem=send_sem,
        recv_sem=recv_sem,
        device_id=device,
        device_id_type=MESH,
    )


def kernel(
    dims,
    order_ref,
    counts_ref,
    mask_ref,
    q_ref,
    nk_ref,
    nv_ref,
    ck_ref,
    cv_ref,
    out_ref,
    qbuf,
    qx,
    kv,
    kx,
    acc,
    run_max,
    score_a,
    score_b,
    max_a,
    max_b,
    obuf,
    kv_send,
    kv_recv,
    q_send,
    q_recv,
    ring_send,
    ring_recv,
    out_send,
    out_recv,
):
    n_ctx, n_head, rows, per_group = dims
    chips = n_ctx // 2
    half = chips // 2
    block = rows * n_head
    pair_keys = 2 * block
    q_cols = per_group * HD
    s = lax.axis_index("section")
    c = lax.axis_index("ctx")
    h = lax.axis_index("head")
    other = 1 - s
    z = c // 2
    core = c % 2
    sib = (s, 2 * z + 1 - core, h)
    up = (s, lax.rem(c + 2, n_ctx), h)
    down = (s, lax.rem(c + n_ctx - 2, n_ctx), h)

    def peer(d):
        return lax.rem(h + d, n_head)

    def head_rows(number):
        return pl.ds(pl.multiple_of(number * rows, rows), rows)

    def head_cols(number, width):
        return pl.ds(pl.multiple_of(number * width, width), width)

    def block_rows(number):
        return pl.ds(pl.multiple_of(number * block, block), block)

    barrier = pltpu.get_barrier_semaphore()
    greeted = [(s, c, peer(d)) for d in range(1, n_head)]
    greeted += [(other, c, peer(d)) for d in range(n_head)]
    greeted += [sib, up, down]
    for device in greeted:
        pl.semaphore_signal(barrier, inc=1, device_id=device, device_id_type=MESH)
    pl.semaphore_wait(barrier, len(greeted))

    mine = pl.ds(pl.multiple_of(c * block + h * rows, rows), rows)
    locals_kv, sends_kv = [], []
    for a, ref in enumerate((nk_ref, nv_ref)):
        copy = pltpu.make_async_copy(
            ref.at[0, :, head_cols(h, HD)], kv.at[a, mine, :], kv_recv.at[0]
        )
        copy.start()
        for d in range(1, n_head):
            copy = remote(
                ref.at[0, :, head_cols(peer(d), HD)],
                kv.at[a, mine, :],
                kv_send.at[a, d],
                kv_recv.at[0],
                (s, c, peer(d)),
            )
            copy.start()
            sends_kv.append(copy)
    for a, ref in ((2, ck_ref), (3, cv_ref)):
        for d in range(n_head):
            copy = remote(
                ref.at[0, :, head_cols(peer(d), HD)],
                kv.at[a, mine, :],
                kv_send.at[a, d],
                kv_recv.at[1],
                (other, c, peer(d)),
            )
            copy.start()
            sends_kv.append(copy)

    def part_view(b, part):
        return kv.at[pl.ds(2 * part, 2), block_rows(b), :]

    def ring_copy(b, part, device, slot):
        view = part_view(b, part)
        return remote(view, view, ring_send.at[slot], ring_recv.at[b, part], device)

    def arrived(b, part):
        view = part_view(b, part)
        pltpu.make_async_copy(view, view, ring_recv.at[b, part]).wait()

    def from_down(i):
        return lax.rem(c + n_ctx - 2 * i, n_ctx)

    def from_up(i):
        return lax.rem(c + 2 * i, n_ctx)

    def slot_of(part, way, i):
        return (part * 4 + way) * (half + 1) + i

    def start_own(part):
        for way, device in ((0, up), (1, down), (2, sib)):
            ring_copy(c, part, device, slot_of(part, way, 0)).start()

    def pass_on(i, part, came_up):
        if came_up:
            b = from_down(i)
            arrived(b, part)
            if i < half - 1 or (i == half - 1 and part == 0):
                ring_copy(b, part, up, slot_of(part, 0, i)).start()
            ring_copy(b, part, sib, slot_of(part, 2, i)).start()
        else:
            b = from_up(i)
            arrived(b, part)
            if i < half - 1 or (i == half - 1 and part == 1):
                ring_copy(b, part, down, slot_of(part, 1, i)).start()
            ring_copy(b, part, sib, slot_of(part, 3, i)).start()

    def sib_arrived(delta):
        b = 2 * lax.rem(z + delta + chips, chips) + 1 - core
        arrived(b, 0)
        arrived(b, 1)

    for part in range(2):
        view = part_view(c, part)
        pltpu.make_async_copy(view, view, kv_recv.at[part]).wait()
        start_own(part)

    q_mine = head_rows(h)
    pltpu.make_async_copy(
        q_ref.at[0, :, head_cols(h, q_cols)], qbuf.at[q_mine, :], q_recv
    ).start()
    sends_q = []
    for d in range(1, n_head):
        copy = remote(
            q_ref.at[0, :, head_cols(peer(d), q_cols)],
            qbuf.at[q_mine, :],
            q_send.at[d],
            q_recv,
            (s, c, peer(d)),
        )
        copy.start()
        sends_q.append(copy)

    lane = lax.broadcasted_iota(jnp.int32, (TILE, HD), 1)
    row = lax.broadcasted_iota(jnp.int32, (TILE, HD), 0)
    tiles = rows * n_head // TILE
    for t in range(tiles):
        qx[t * TILE:(t + 1) * TILE, :] = jnp.where(lane == t, 1.0, 0.0).astype(jnp.bfloat16)
    acc[...] = jnp.zeros_like(acc)
    run_max[...] = jnp.full_like(run_max, CLOSED)
    far_order = jnp.full((TILE, HD), order_ref[other], jnp.int32)
    own_order = jnp.full((TILE, HD), order_ref[s], jnp.int32)
    earlier = jnp.where(far_order < own_order, 1, 0)

    def mask_tile(k, _):
        at = pl.ds(pl.multiple_of(k * TILE, TILE), TILE)
        seen = jnp.zeros((TILE, HD), jnp.int32)
        for t in range(tiles):
            seen = jnp.where(lane == t, mask_ref[s, tiles * c + t, k], seen)
        limit = jnp.where(seen > 0, counts_ref[s, k], 0)
        kx[0, at, :] = jnp.where((lane < tiles) & (row >= limit), CLOSED, 0.0).astype(jnp.bfloat16)
        limit = earlier * counts_ref[other, k]
        kx[1, at, :] = jnp.where((lane < tiles) & (row >= limit), CLOSED, 0.0).astype(jnp.bfloat16)
        return 0

    lax.fori_loop(0, n_ctx * tiles, mask_tile, 0)

    pass_on(1, 0, True)
    pass_on(1, 0, False)
    pltpu.make_async_copy(qbuf, qbuf, q_recv).wait()
    sib_arrived(0)

    def pair_rows(j):
        delta = ((j + 1) // 2) * (1 - 2 * (j % 2))
        chip = lax.rem(z + delta + chips, chips)
        return pl.ds(pl.multiple_of(chip * pair_keys, pair_keys), pair_keys)

    def scores(it, score_ref, max_ref):
        at = pair_rows(it // per_group)
        lhs = jnp.concatenate([qbuf[:, head_cols(it % per_group, HD)], qx[...]], 1)
        top = None
        for a in range(2):
            keys = jnp.concatenate([kv[2 * a, at, :], kx[a, at, :]], 1)
            found = lax.dot_general(
                lhs, keys, (((1,), (1,)), ((), ())), preferred_element_type=jnp.float32
            )
            score_ref[:, a * pair_keys:(a + 1) * pair_keys] = found
            for t in range(pair_keys // HD):
                piece = found[:, t * HD:(t + 1) * HD]
                top = piece if top is None else jnp.maximum(top, piece)
        max_ref[...] = top

    def fold(it, score_ref, max_ref):
        at = pair_rows(it // per_group)
        head = it % per_group
        old = run_max[head]
        new = jnp.maximum(old, jnp.max(max_ref[...], axis=1, keepdims=True))
        factor = jnp.exp2((old - new) * EXP_SCALE)
        run_max[head] = new
        ones = jnp.ones((pair_keys, HD), jnp.bfloat16)
        added = None
        for a in range(2):
            pieces = []
            for t in range(pair_keys // HD):
                first = a * pair_keys + t * HD
                piece = score_ref[:, first:first + HD]
                pieces.append(jnp.exp2((piece - new) * EXP_SCALE).astype(jnp.bfloat16))
            weights = jnp.concatenate(pieces, 1)
            values = jnp.concatenate([kv[2 * a + 1, at, :], ones], 1)
            term = jnp.dot(weights, values, preferred_element_type=jnp.float32)
            added = term if added is None else added + term
        acc[head] = acc[head] * jnp.concatenate([factor, factor], 1) + added

    def out_copy(head, d):
        there = peer(d)
        return remote(
            obuf.at[head, head_rows(there), :],
            out_ref.at[0, :, head_cols(h * per_group + head, HD)],
            out_send.at[head, d],
            out_recv,
            (s, c, there),
        )

    def finish(head):
        total = acc[head]
        obuf[head] = (total[:, :HD] / total[:, HD:]).astype(jnp.bfloat16)
        pltpu.make_async_copy(
            obuf.at[head, head_rows(h), :],
            out_ref.at[0, :, head_cols(h * per_group + head, HD)],
            out_recv,
        ).start()
        for d in range(1, n_head):
            out_copy(head, d).start()

    total_its = per_group * chips
    actions = {}

    def at_it(it, action):
        actions.setdefault(it // 2, []).append(action)

    at_it(3, lambda: (pass_on(1, 1, True), pass_on(1, 1, False)))
    for i in range(1, half):
        first = (2 * i - 1) * per_group
        at_it(first - 1, functools.partial(sib_arrived, -i))
        at_it(first + 5, functools.partial(sib_arrived, i))
        if i < half - 1:
            at_it(first + 3, lambda i=i: (pass_on(i + 1, 0, True), pass_on(i + 1, 0, False)))
            at_it(first + 9, lambda i=i: (pass_on(i + 1, 1, True), pass_on(i + 1, 1, False)))
        else:
            at_it(first + 3, lambda: (pass_on(half, 0, True), pass_on(half, 1, False)))
    at_it((2 * half - 1) * per_group - 1, functools.partial(sib_arrived, half))

    scores(0, score_a, max_a)

    def step(k, _):
        scores(2 * k + 1, score_b, max_b)
        fold(2 * k, score_a, max_a)

        @pl.when(k >= (total_its - per_group) // 2)
        def _():
            finish((2 * k) % per_group)

        for at, todo in sorted(actions.items()):

            @pl.when(k == at)
            def _(todo=todo):
                for action in todo:
                    action()

        scores(lax.rem(2 * k + 2, total_its), score_a, max_a)
        fold(2 * k + 1, score_b, max_b)

        @pl.when(k >= (total_its - per_group) // 2)
        def _():
            finish((2 * k + 1) % per_group)

        return 0

    lax.fori_loop(0, total_its // 2, step, 0)

    for copy in sends_kv + sends_q:
        copy.wait_send()
    for part in range(2):
        for way in (0, 1):
            last = half if part == way else half - 1
            for i in range(last):
                ring_copy(c, part, up, slot_of(part, way, i)).wait_send()
        ring_copy(c, part, sib, slot_of(part, 2, 0)).wait_send()
        for i in range(1, half + 1):
            for way in (2, 3):
                if i < half or way == 2 + part:
                    ring_copy(c, part, sib, slot_of(part, way, i)).wait_send()
    for head in range(per_group):
        for d in range(1, n_head):
            out_copy(head, d).wait_send()
    pltpu.make_async_copy(out_ref, out_ref, out_recv).wait()


def local(
    queries, noisy_keys, noisy_values, clean_keys, clean_values, clip_order, key_counts, tile_mask
):
    n_ctx = lax.axis_size("ctx")
    n_head = lax.axis_size("head")
    rows = queries.shape[1]
    groups = noisy_keys.shape[2] // HD
    heads = queries.shape[2] // HD
    per_group = heads // groups
    block = rows * n_head
    keys = block * n_ctx
    half = n_ctx // 4
    score = pltpu.VMEM((block, 4 * block), jnp.float32)
    smem = pl.BlockSpec(memory_space=pltpu.SMEM)
    anywhere = pl.BlockSpec(memory_space=pl.ANY)
    return pl.pallas_call(
        functools.partial(kernel, (n_ctx, n_head, rows, per_group)),
        out_shape=jax.ShapeDtypeStruct(queries.shape, queries.dtype),
        in_specs=[smem] * 3 + [anywhere] * 5,
        out_specs=anywhere,
        scratch_shapes=[
            pltpu.VMEM((block, per_group * HD), jnp.bfloat16),
            pltpu.VMEM((block, HD), jnp.bfloat16),
            pltpu.VMEM((4, keys, HD), jnp.bfloat16),
            pltpu.VMEM((2, keys, HD), jnp.bfloat16),
            pltpu.VMEM((per_group, block, 2 * HD), jnp.float32),
            pltpu.VMEM((per_group, block, HD), jnp.float32),
            score,
            score,
            pltpu.VMEM((block, HD), jnp.float32),
            pltpu.VMEM((block, HD), jnp.float32),
            pltpu.VMEM((per_group, block, HD), jnp.bfloat16),
            pltpu.SemaphoreType.DMA((4, n_head)),
            pltpu.SemaphoreType.DMA((2,)),
            pltpu.SemaphoreType.DMA((n_head,)),
            pltpu.SemaphoreType.DMA,
            pltpu.SemaphoreType.DMA((8 * (half + 1),)),
            pltpu.SemaphoreType.DMA((n_ctx, 2)),
            pltpu.SemaphoreType.DMA((per_group, n_head)),
            pltpu.SemaphoreType.DMA,
        ],
        compiler_params=pltpu.CompilerParams(
            collective_id=0, has_side_effects=True, vmem_limit_bytes=48 * 2**20
        ),
        cost_estimate=pl.CostEstimate(
            flops=4 * block * per_group * 2 * keys * HD,
            bytes_accessed=2**22,
            transcendentals=block * per_group * 2 * keys,
        ),
        name="attend",
    )(
        clip_order,
        key_counts,
        tile_mask,
        queries,
        noisy_keys,
        noisy_values,
        clean_keys,
        clean_values,
    )


def solution(mesh):
    split = P("section", ("ctx", "head"), None)
    return jax.shard_map(
        local,
        mesh=mesh,
        in_specs=(split,) * 5 + (P(),) * 3,
        out_specs=split,
        check_vma=False,
    )
```

```python
import functools
import math

import jax
import jax.numpy as jnp
from jax import lax
from jax.experimental import pallas as pl
from jax.experimental.pallas import tpu as pltpu
from jax.sharding import PartitionSpec as P

MESH = pl.DeviceIdType.MESH
HD = 128
TILE = 128
CLOSED = -1e30
EXP_SCALE = math.log2(math.e) * HD ** -0.5


def remote(src, dst, send_sem, recv_sem, device):
    return pltpu.make_async_remote_copy(
        src_ref=src,
        dst_ref=dst,
        send_sem=send_sem,
        recv_sem=recv_sem,
        device_id=device,
        device_id_type=MESH,
    )


def kernel(
    dims,
    order_hbm,
    counts_hbm,
    mask_hbm,
    q_ref,
    nk_ref,
    nv_ref,
    ck_ref,
    cv_ref,
    out_ref,
    order_ref,
    counts_ref,
    mask_ref,
    stage_kv,
    stage_q,
    qbuf,
    qcat,
    kv,
    kx,
    acc,
    run_max,
    score_a,
    score_b,
    max_a,
    max_b,
    obuf,
    load_sem,
    kv_send,
    kv_recv,
    q_send,
    q_recv,
    ring_send,
    ring_recv,
    out_send,
    out_recv,
):
    n_ctx, n_head, rows, per_group = dims
    chips = n_ctx // 2
    half = chips // 2
    block = rows * n_head
    pair_keys = 2 * block
    q_cols = per_group * HD
    tiles = block // TILE
    s = lax.axis_index("section")
    c = lax.axis_index("ctx")
    h = lax.axis_index("head")
    other = 1 - s
    z = c // 2
    core = c % 2
    sib = (s, 2 * z + 1 - core, h)
    up = (s, lax.rem(c + 2, n_ctx), h)
    down = (s, lax.rem(c + n_ctx - 2, n_ctx), h)

    def peer(d):
        return lax.rem(h + d, n_head)

    def head_rows(number):
        return pl.ds(pl.multiple_of(number * rows, rows), rows)

    def head_cols(number, width):
        return pl.ds(pl.multiple_of(number * width, width), width)

    def block_rows(number):
        return pl.ds(pl.multiple_of(number * block, block), block)

    loads = [
        pltpu.make_async_copy(ref.at[0], stage_kv.at[a], load_sem.at[a])
        for a, ref in enumerate((nk_ref, nv_ref, ck_ref, cv_ref))
    ]
    loads.append(pltpu.make_async_copy(q_ref.at[0], stage_q, load_sem.at[4]))
    tables = ((order_hbm, order_ref), (counts_hbm, counts_ref), (mask_hbm, mask_ref))
    for a, (src, dst) in enumerate(tables):
        loads.append(pltpu.make_async_copy(src, dst, load_sem.at[5 + a]))
    for copy in loads:
        copy.start()

    barrier = pltpu.get_barrier_semaphore()
    greeted = [(s, c, peer(d)) for d in range(1, n_head)]
    greeted += [(other, c, peer(d)) for d in range(n_head)]
    greeted += [sib, up, down]
    for device in greeted:
        pl.semaphore_signal(barrier, inc=1, device_id=device, device_id_type=MESH)
    for copy in loads[:4]:
        copy.wait()
    pl.semaphore_wait(barrier, len(greeted))

    mine = pl.ds(pl.multiple_of(c * block + h * rows, rows), rows)
    sends = []

    def send_kv(part, d, device):
        copy = remote(
            stage_kv.at[2 * part:2 * part + 2, :, head_cols(peer(d), HD)],
            kv.at[2 * part:2 * part + 2, mine, :],
            kv_send.at[part, d],
            kv_recv.at[part],
            device,
        )
        copy.start()
        sends.append(copy)

    for d in range(1, n_head):
        send_kv(0, d, (s, c, peer(d)))
    pltpu.make_async_copy(
        stage_kv.at[0:2, :, head_cols(h, HD)], kv.at[0:2, mine, :], kv_recv.at[0]
    ).start()
    for d in range(n_head):
        send_kv(1, d, (other, c, peer(d)))

    loads[4].wait()
    q_mine = head_rows(h)
    for d in range(1, n_head):
        copy = remote(
            stage_q.at[:, head_cols(peer(d), q_cols)],
            qbuf.at[q_mine, :],
            q_send.at[d],
            q_recv,
            (s, c, peer(d)),
        )
        copy.start()
        sends.append(copy)
    pltpu.make_async_copy(
        stage_q.at[:, head_cols(h, q_cols)], qbuf.at[q_mine, :], q_recv
    ).start()

    def part_view(b, part):
        return kv.at[pl.ds(2 * part, 2), block_rows(b), :]

    def ring_copy(b, part, device, slot):
        view = part_view(b, part)
        return remote(view, view, ring_send.at[slot], ring_recv.at[b, part], device)

    def arrived(b, part):
        view = part_view(b, part)
        pltpu.make_async_copy(view, view, ring_recv.at[b, part]).wait()

    def slot_of(part, way, i):
        return (part * 4 + way) * (half + 1) + i

    def pass_on(i, part, came_up):
        if came_up:
            b = lax.rem(c + n_ctx - 2 * i, n_ctx)
            arrived(b, part)
            if i < half - 1 or (i == half - 1 and part == 0):
                ring_copy(b, part, up, slot_of(part, 0, i)).start()
            ring_copy(b, part, sib, slot_of(part, 2, i)).start()
        else:
            b = lax.rem(c + 2 * i, n_ctx)
            arrived(b, part)
            if i < half - 1 or (i == half - 1 and part == 1):
                ring_copy(b, part, down, slot_of(part, 1, i)).start()
            ring_copy(b, part, sib, slot_of(part, 3, i)).start()

    def pass_both(number):
        i, part = (number + 1) // 2, (number + 1) % 2
        pass_on(i, part, True)
        pass_on(i, part if i < half else 1, False)

    def sib_arrived(delta, part):
        chip = lax.rem(z + delta + chips, chips)
        arrived(2 * chip + 1 - core, part)

    for part in range(2):
        view = part_view(c, part)
        pltpu.make_async_copy(view, view, kv_recv.at[part]).wait()
        for way, device in ((0, up), (1, down), (2, sib)):
            ring_copy(c, part, device, slot_of(part, way, 0)).start()

    lane = lax.broadcasted_iota(jnp.int32, (TILE, HD), 1)
    row = lax.broadcasted_iota(jnp.int32, (TILE, HD), 0)
    for head in range(per_group):
        for t in range(tiles):
            first = head * block + t * TILE
            qcat[first:first + TILE, HD:] = jnp.where(lane == t, 1.0, 0.0).astype(jnp.bfloat16)
    acc[...] = jnp.zeros_like(acc)
    run_max[...] = jnp.full_like(run_max, CLOSED)
    for copy in loads[5:]:
        copy.wait()
    far_order = jnp.full((TILE, HD), order_ref[other], jnp.int32)
    own_order = jnp.full((TILE, HD), order_ref[s], jnp.int32)
    earlier = jnp.where(far_order < own_order, 1, 0)

    def mask_tile(k, _):
        at = pl.ds(pl.multiple_of(k * TILE, TILE), TILE)
        seen = jnp.zeros((TILE, HD), jnp.int32)
        for t in range(tiles):
            seen = jnp.where(lane == t, mask_ref[s, tiles * c + t, k], seen)
        limit = jnp.where(seen > 0, counts_ref[s, k], 0)
        kx[0, at, :] = jnp.where((lane < tiles) & (row >= limit), CLOSED, 0.0).astype(jnp.bfloat16)
        limit = earlier * counts_ref[other, k]
        kx[1, at, :] = jnp.where((lane < tiles) & (row >= limit), CLOSED, 0.0).astype(jnp.bfloat16)
        return 0

    lax.fori_loop(0, n_ctx * tiles, mask_tile, 0)

    pass_both(1)
    pltpu.make_async_copy(qbuf, qbuf, q_recv).wait()
    for head in range(per_group):
        qcat[head * block:(head + 1) * block, :HD] = qbuf[:, head * HD:(head + 1) * HD]
    sib_arrived(0, 0)
    sib_arrived(0, 1)

    def chunk(k, second):
        i, part = (k + 1) // 2, (k + 1) % 2
        if second:
            alone = (half - i % half) // half
            part = (part + alone) % 2
            chip = lax.rem(z + i, chips)
        else:
            chip = lax.rem(z + chips - i, chips)
        return part, pl.ds(pl.multiple_of(chip * pair_keys, pair_keys), pair_keys)

    def scores(where, score_ref, max_ref):
        part, at = where
        keys = jnp.concatenate([kv[2 * part, at, :], kx[part, at, :]], 1)
        found = lax.dot_general(
            qcat[...], keys, (((1,), (1,)), ((), ())), preferred_element_type=jnp.float32
        )
        score_ref[...] = found
        top = found[:, :HD]
        for t in range(1, pair_keys // HD):
            top = jnp.maximum(top, found[:, t * HD:(t + 1) * HD])
        max_ref[...] = top

    def fold(where, score_ref, max_ref):
        part, at = where
        old = run_max[...]
        new = jnp.maximum(old, jnp.max(max_ref[...], axis=1, keepdims=True))
        factor = jnp.exp2((old - new) * EXP_SCALE)
        run_max[...] = new
        pieces = []
        for t in range(pair_keys // HD):
            piece = score_ref[:, t * HD:(t + 1) * HD]
            pieces.append(jnp.exp2((piece - new) * EXP_SCALE).astype(jnp.bfloat16))
        weights = jnp.concatenate(pieces, 1)
        ones = jnp.ones((pair_keys, HD), jnp.bfloat16)
        values = jnp.concatenate([kv[2 * part + 1, at, :], ones], 1)
        added = jnp.dot(weights, values, preferred_element_type=jnp.float32)
        acc[...] = acc[...] * jnp.concatenate([factor, factor], 1) + added

    scores(chunk(0, False), score_a, max_a)

    def step(k, _):
        for number in range(2, 2 * half):

            @pl.when(k == number - 1)
            def _(number=number):
                pass_both(number)

        for number in range(1, 2 * half):

            @pl.when(k == number)
            def _(number=number):
                if number < 2 * half - 1:
                    sib_arrived((number + 1) // 2, (number + 1) % 2)
                else:
                    sib_arrived(half, 1)

        scores(chunk(k, True), score_b, max_b)
        fold(chunk(k, False), score_a, max_a)

        for number in range(1, 2 * half):

            @pl.when(k == number - 1)
            def _(number=number):
                sib_arrived(-((number + 1) // 2), (number + 1) % 2)

        scores(chunk(lax.rem(k + 1, 2 * half), False), score_a, max_a)
        fold(chunk(k, True), score_b, max_b)
        return 0

    lax.fori_loop(0, 2 * half, step, 0)

    out_cols = head_cols(h, q_cols)

    def finish(there):
        for head in range(per_group):
            at = pl.ds(pl.multiple_of(head * block + there * rows, rows), rows)
            total = acc[at, :]
            obuf[head_rows(there), head * HD:(head + 1) * HD] = (
                total[:, :HD] / total[:, HD:]
            ).astype(jnp.bfloat16)

    for d in range(1, n_head):
        there = peer(d)
        finish(there)
        copy = remote(
            obuf.at[head_rows(there), :],
            out_ref.at[0, :, out_cols],
            out_send.at[d],
            out_recv,
            (s, c, there),
        )
        copy.start()
        sends.append(copy)
    finish(h)
    pltpu.make_async_copy(obuf.at[head_rows(h), :], out_ref.at[0, :, out_cols], out_recv).start()

    for copy in sends:
        copy.wait_send()
    for part in range(2):
        for way in (0, 1):
            for i in range(half if part == way else half - 1):
                ring_copy(c, part, up, slot_of(part, way, i)).wait_send()
        ring_copy(c, part, sib, slot_of(part, 2, 0)).wait_send()
        for i in range(1, half + 1):
            for way in (2, 3):
                if i < half or way == 2 + part:
                    ring_copy(c, part, sib, slot_of(part, way, i)).wait_send()
    pltpu.make_async_copy(out_ref, out_ref, out_recv).wait()


def local(
    queries, noisy_keys, noisy_values, clean_keys, clean_values, clip_order, key_counts, tile_mask
):
    n_ctx = lax.axis_size("ctx")
    n_head = lax.axis_size("head")
    rows = queries.shape[1]
    groups = noisy_keys.shape[2] // HD
    heads = queries.shape[2] // HD
    per_group = heads // groups
    block = rows * n_head
    keys = block * n_ctx
    half = n_ctx // 4
    bf16, f32 = jnp.bfloat16, jnp.float32
    all_rows = per_group * block
    anywhere = pl.BlockSpec(memory_space=pl.ANY)
    return pl.pallas_call(
        functools.partial(kernel, (n_ctx, n_head, rows, per_group)),
        out_shape=jax.ShapeDtypeStruct(queries.shape, queries.dtype),
        in_specs=[anywhere] * 8,
        out_specs=anywhere,
        scratch_shapes=[
            pltpu.SMEM(clip_order.shape, jnp.int32),
            pltpu.SMEM(key_counts.shape, jnp.int32),
            pltpu.SMEM(tile_mask.shape, jnp.int32),
            pltpu.VMEM((4, rows, groups * HD), bf16),
            pltpu.VMEM((rows, heads * HD), bf16),
            pltpu.VMEM((block, per_group * HD), bf16),
            pltpu.VMEM((all_rows, 2 * HD), bf16),
            pltpu.VMEM((4, keys, HD), bf16),
            pltpu.VMEM((2, keys, HD), bf16),
            pltpu.VMEM((all_rows, 2 * HD), f32),
            pltpu.VMEM((all_rows, HD), f32),
            pltpu.VMEM((all_rows, 2 * block), f32),
            pltpu.VMEM((all_rows, 2 * block), f32),
            pltpu.VMEM((all_rows, HD), f32),
            pltpu.VMEM((all_rows, HD), f32),
            pltpu.VMEM((block, per_group * HD), bf16),
            pltpu.SemaphoreType.DMA((8,)),
            pltpu.SemaphoreType.DMA((2, n_head)),
            pltpu.SemaphoreType.DMA((2,)),
            pltpu.SemaphoreType.DMA((n_head,)),
            pltpu.SemaphoreType.DMA,
            pltpu.SemaphoreType.DMA((8 * (half + 1),)),
            pltpu.SemaphoreType.DMA((n_ctx, 2)),
            pltpu.SemaphoreType.DMA((n_head,)),
            pltpu.SemaphoreType.DMA,
        ],
        compiler_params=pltpu.CompilerParams(
            collective_id=0, has_side_effects=True, vmem_limit_bytes=60 * 2**20
        ),
        cost_estimate=pl.CostEstimate(
            flops=4 * all_rows * 2 * keys * HD,
            bytes_accessed=2**22,
            transcendentals=all_rows * 2 * keys,
        ),
        name="attend",
    )(
        clip_order,
        key_counts,
        tile_mask,
        queries,
        noisy_keys,
        noisy_values,
        clean_keys,
        clean_values,
    )


def solution(mesh):
    split = P("section", ("ctx", "head"), None)
    return jax.shard_map(
        local,
        mesh=mesh,
        in_specs=(split,) * 5 + (P(),) * 3,
        out_specs=split,
        check_vma=False,
    )
```

```python
import functools
import math

import jax
import jax.numpy as jnp
from jax import lax
from jax.experimental import pallas as pl
from jax.experimental.pallas import tpu as pltpu
from jax.sharding import PartitionSpec as P

MESH = pl.DeviceIdType.MESH
HD = 128
TILE = 128
CLOSED = -1e30
EXP_SCALE = math.log2(math.e) * HD ** -0.5


def remote(src, dst, send_sem, recv_sem, device):
    return pltpu.make_async_remote_copy(
        src_ref=src,
        dst_ref=dst,
        send_sem=send_sem,
        recv_sem=recv_sem,
        device_id=device,
        device_id_type=MESH,
    )


def kernel(
    dims,
    order_hbm,
    counts_hbm,
    mask_hbm,
    q_ref,
    nk_ref,
    nv_ref,
    ck_ref,
    cv_ref,
    out_ref,
    order_ref,
    counts_ref,
    mask_ref,
    stage_kv,
    stage_q,
    qbuf,
    qcat,
    kv,
    kx,
    acc,
    run_max,
    score_a,
    score_b,
    max_a,
    max_b,
    obuf,
    load_sem,
    kv_send,
    kv_recv,
    q_send,
    q_recv,
    ring_send,
    ring_recv,
    out_send,
    out_recv,
):
    n_ctx, n_head, rows, per_group = dims
    chips = n_ctx // 2
    half = chips // 2
    block = rows * n_head
    pair_keys = 2 * block
    q_cols = per_group * HD
    tiles = block // TILE
    s = lax.axis_index("section")
    c = lax.axis_index("ctx")
    h = lax.axis_index("head")
    other = 1 - s
    z = c // 2
    core = c % 2
    sib = (s, 2 * z + 1 - core, h)
    up = (s, lax.rem(c + 2, n_ctx), h)
    down = (s, lax.rem(c + n_ctx - 2, n_ctx), h)

    def peer(d):
        return lax.rem(h + d, n_head)

    def head_rows(number):
        return pl.ds(pl.multiple_of(number * rows, rows), rows)

    def head_cols(number, width):
        return pl.ds(pl.multiple_of(number * width, width), width)

    def block_rows(number):
        return pl.ds(pl.multiple_of(number * block, block), block)

    for a, ref in enumerate((nk_ref, nv_ref, ck_ref, cv_ref)):
        pltpu.make_async_copy(ref.at[0], stage_kv.at[a], load_sem.at[0]).start()
    load_q = pltpu.make_async_copy(q_ref.at[0], stage_q, load_sem.at[1])
    load_q.start()
    load_tables = [
        pltpu.make_async_copy(order_hbm, order_ref, load_sem.at[2]),
        pltpu.make_async_copy(counts_hbm, counts_ref, load_sem.at[3]),
        pltpu.make_async_copy(mask_hbm, mask_ref, load_sem.at[4]),
    ]
    for copy in load_tables:
        copy.start()

    barrier = pltpu.get_barrier_semaphore()
    greeted = [(s, c, peer(d)) for d in range(1, n_head)]
    greeted += [(other, c, peer(d)) for d in range(n_head)]
    greeted += [sib, up, down]
    for device in greeted:
        pl.semaphore_signal(barrier, inc=1, device_id=device, device_id_type=MESH)
    pltpu.make_async_copy(stage_kv, stage_kv, load_sem.at[0]).wait()
    pl.semaphore_wait(barrier, len(greeted))

    mine = pl.ds(pl.multiple_of(c * block + h * rows, rows), rows)

    def send_kv(part, d, device):
        copy = remote(
            stage_kv.at[2 * part:2 * part + 2, :, head_cols(peer(d), HD)],
            kv.at[2 * part:2 * part + 2, mine, :],
            kv_send,
            kv_recv.at[part],
            device,
        )
        copy.start()

    for d in range(1, n_head):
        send_kv(0, d, (s, c, peer(d)))
    pltpu.make_async_copy(
        stage_kv.at[0:2, :, head_cols(h, HD)], kv.at[0:2, mine, :], kv_recv.at[0]
    ).start()
    for d in range(n_head):
        send_kv(1, d, (other, c, peer(d)))

    load_q.wait()
    q_mine = head_rows(h)
    for d in range(1, n_head):
        copy = remote(
            stage_q.at[:, head_cols(peer(d), q_cols)],
            qbuf.at[q_mine, :],
            q_send,
            q_recv,
            (s, c, peer(d)),
        )
        copy.start()
    pltpu.make_async_copy(
        stage_q.at[:, head_cols(h, q_cols)], qbuf.at[q_mine, :], q_recv
    ).start()

    def view(b, part):
        return kv.at[pl.ds(2 * part, 2), block_rows(b), :]

    def arrived(b, part):
        pltpu.make_async_copy(view(b, part), view(b, part), ring_recv.at[b, part]).wait()

    def ring_block(i, way):
        if way == "up":
            return lax.rem(c + n_ctx - 2 * i, n_ctx)
        return lax.rem(c + 2 * i, n_ctx)

    plans = {}
    for i in range(half + 1):
        for part in range(2):
            for number, (way, device) in enumerate((("up", up), ("down", down))):
                if i < half:
                    plans[way, i, part] = number, device
                if 0 < i < half or way == "up":
                    plans["sib", way, i, part] = 2, sib

    def copy_of(*name):
        number, device = plans[name]
        way, i, part = name[-3:]
        b = ring_block(i, way)
        piece = view(b, part)
        if name[0] != "sib" and i == half - 1:
            piece = piece.at[0:1] if way == "up" else piece.at[1:2]
        return remote(piece, piece, ring_send.at[number], ring_recv.at[b, part], device)

    def spread(i, way, part):
        for name in ((way, i, part), ("sib", way, i, part)):
            if name in plans:
                copy_of(*name).start()

    def from_ring(i, part):
        for way in ("up", "down"):
            if ("sib", way, i, part) in plans:
                arrived(ring_block(i, way), part)
                spread(i, way, part)

    def from_sib(delta, part):
        chip = lax.rem(z + delta + chips, chips)
        arrived(2 * chip + 1 - core, part)

    for part in range(2):
        both = kv.at[2 * part:2 * part + 2, block_rows(c), :]
        pltpu.make_async_copy(both, both, kv_recv.at[part]).wait()
        spread(0, "down", part)
        spread(0, "up", part)

    lane = lax.broadcasted_iota(jnp.int32, (TILE, HD), 1)
    row = lax.broadcasted_iota(jnp.int32, (TILE, HD), 0)
    for head in range(per_group):
        for t in range(tiles):
            first = head * block + t * TILE
            qcat[first:first + TILE, HD:] = jnp.where(lane == t, 1.0, 0.0).astype(jnp.bfloat16)
    acc[...] = jnp.zeros_like(acc)
    run_max[...] = jnp.full_like(run_max, CLOSED)
    for copy in load_tables:
        copy.wait()
    far_order = jnp.full((TILE, HD), order_ref[other], jnp.int32)
    own_order = jnp.full((TILE, HD), order_ref[s], jnp.int32)
    earlier = jnp.where(far_order < own_order, 1, 0)

    def mask_tile(k, _):
        at = pl.ds(pl.multiple_of(k * TILE, TILE), TILE)
        seen = jnp.zeros((TILE, HD), jnp.int32)
        for t in range(tiles):
            seen = jnp.where(lane == t, mask_ref[s, tiles * c + t, k], seen)
        limit = jnp.where(seen > 0, counts_ref[s, k], 0)
        kx[0, at, :] = jnp.where((lane < tiles) & (row >= limit), CLOSED, 0.0).astype(jnp.bfloat16)
        limit = earlier * counts_ref[other, k]
        kx[1, at, :] = jnp.where((lane < tiles) & (row >= limit), CLOSED, 0.0).astype(jnp.bfloat16)
        return 0

    lax.fori_loop(0, n_ctx * tiles, mask_tile, 0)

    from_ring(1, 0)
    pltpu.make_async_copy(qbuf, qbuf, q_recv).wait()
    for head in range(per_group):
        qcat[head * block:(head + 1) * block, :HD] = qbuf[:, head * HD:(head + 1) * HD]
    from_sib(0, 0)

    def chunk(n):
        i, r = (n + 2) // 4, (n + 2) % 4
        alone = (half - i % half) // half
        part = (1 - alone) * (r // 2) + alone * (r % 2)
        chip = lax.rem(z + chips + i * (2 * (r % 2) - 1), chips)
        return part, pl.ds(pl.multiple_of(chip * pair_keys, pair_keys), pair_keys)

    def scores(where, score_ref, max_ref):
        part, at = where
        keys = jnp.concatenate([kv[2 * part, at, :], kx[part, at, :]], 1)
        found = lax.dot_general(
            qcat[...], keys, (((1,), (1,)), ((), ())), preferred_element_type=jnp.float32
        )
        score_ref[...] = found
        top = found[:, :HD]
        for t in range(1, pair_keys // HD):
            top = jnp.maximum(top, found[:, t * HD:(t + 1) * HD])
        max_ref[...] = top

    def fold(where, score_ref, max_ref):
        part, at = where
        old = run_max[...]
        new = jnp.maximum(old, jnp.max(max_ref[...], axis=1, keepdims=True))
        factor = jnp.exp2((old - new) * EXP_SCALE)
        run_max[...] = new
        pieces = []
        for t in range(pair_keys // HD):
            piece = score_ref[:, t * HD:(t + 1) * HD]
            pieces.append(jnp.exp2((piece - new) * EXP_SCALE).astype(jnp.bfloat16))
        weights = jnp.concatenate(pieces, 1)
        ones = jnp.ones((pair_keys, HD), jnp.bfloat16)
        values = jnp.concatenate([kv[2 * part + 1, at, :], ones], 1)
        added = jnp.dot(weights, values, preferred_element_type=jnp.float32)
        acc[...] = acc[...] * jnp.concatenate([factor, factor], 1) + added

    todo = {n: [] for n in range(1, 4 * half)}
    todo[1] += [functools.partial(from_sib, 0, 1)]
    for i in range(1, half + 1):
        first = 4 * i - 2
        for part in range(2):
            if i < half:
                todo[first + 2 * part] += [functools.partial(from_sib, -i, part)]
                todo[first + 2 * part + 1] += [functools.partial(from_sib, i, part)]
            else:
                todo[first + part] += [functools.partial(from_sib, i, part)]
    ring_at = {2: [(1, 1)], 4: [(2, 0)], 6: [(2, 1)], 8: [(3, 0)], 10: [(3, 1)], 11: [(4, 0)], 13: [(4, 1)]}
    for n, events in ring_at.items():
        todo[n] = [functools.partial(from_ring, *event) for event in events] + todo[n]
    scores(chunk(0), score_a, max_a)

    def prepare(k, odd):
        for n, actions in todo.items():
            if n % 2 == odd and n < 4 * half - 1:

                @pl.when(k == (n - odd) // 2)
                def _(actions=actions):
                    for action in actions:
                        action()

    def step(k, _):
        prepare(k, 1)
        scores(chunk(2 * k + 1), score_b, max_b)
        fold(chunk(2 * k), score_a, max_a)
        prepare(k + 1, 0)
        scores(chunk(2 * k + 2), score_a, max_a)
        fold(chunk(2 * k + 1), score_b, max_b)
        return 0

    lax.fori_loop(0, 2 * half - 1, step, 0)
    for action in todo[4 * half - 1]:
        action()
    scores(chunk(4 * half - 1), score_b, max_b)
    fold(chunk(4 * half - 2), score_a, max_a)
    fold(chunk(4 * half - 1), score_b, max_b)

    out_cols = head_cols(h, q_cols)

    def finish(there):
        for head in range(per_group):
            at = pl.ds(pl.multiple_of(head * block + there * rows, rows), rows)
            total = acc[at, :]
            obuf[head_rows(there), head * HD:(head + 1) * HD] = (
                total[:, :HD] / total[:, HD:]
            ).astype(jnp.bfloat16)

    for d in range(1, n_head):
        there = peer(d)
        finish(there)
        copy = remote(
            obuf.at[head_rows(there), :],
            out_ref.at[0, :, out_cols],
            out_send,
            out_recv,
            (s, c, there),
        )
        copy.start()
    finish(h)
    pltpu.make_async_copy(obuf.at[head_rows(h), :], out_ref.at[0, :, out_cols], out_recv).start()

    def drained(view, sem):
        pltpu.make_async_copy(view, view, sem).wait()

    away = block - rows
    drained(kv.at[0:2, 0:2 * block - rows, :], kv_send)
    drained(qbuf.at[0:away, :], q_send)
    along = kv.at[:, 0:(2 * half - 1) * block // 2, :]
    drained(along, ring_send.at[0])
    drained(along, ring_send.at[1])
    drained(kv.at[:, 0:chips * block, :], ring_send.at[2])
    drained(obuf.at[0:away, :], out_send)
    pltpu.make_async_copy(out_ref, out_ref, out_recv).wait()


def local(
    queries, noisy_keys, noisy_values, clean_keys, clean_values, clip_order, key_counts, tile_mask
):
    n_ctx = lax.axis_size("ctx")
    n_head = lax.axis_size("head")
    rows = queries.shape[1]
    groups = noisy_keys.shape[2] // HD
    heads = queries.shape[2] // HD
    per_group = heads // groups
    block = rows * n_head
    keys = block * n_ctx
    half = n_ctx // 4
    bf16, f32 = jnp.bfloat16, jnp.float32
    all_rows = per_group * block
    anywhere = pl.BlockSpec(memory_space=pl.ANY)
    return pl.pallas_call(
        functools.partial(kernel, (n_ctx, n_head, rows, per_group)),
        out_shape=jax.ShapeDtypeStruct(queries.shape, queries.dtype),
        in_specs=[anywhere] * 8,
        out_specs=anywhere,
        scratch_shapes=[
            pltpu.SMEM(clip_order.shape, jnp.int32),
            pltpu.SMEM(key_counts.shape, jnp.int32),
            pltpu.SMEM(tile_mask.shape, jnp.int32),
            pltpu.VMEM((4, rows, groups * HD), bf16),
            pltpu.VMEM((rows, heads * HD), bf16),
            pltpu.VMEM((block, per_group * HD), bf16),
            pltpu.VMEM((all_rows, 2 * HD), bf16),
            pltpu.VMEM((4, keys, HD), bf16),
            pltpu.VMEM((2, keys, HD), bf16),
            pltpu.VMEM((all_rows, 2 * HD), f32),
            pltpu.VMEM((all_rows, HD), f32),
            pltpu.VMEM((all_rows, 2 * block), f32),
            pltpu.VMEM((all_rows, 2 * block), f32),
            pltpu.VMEM((all_rows, HD), f32),
            pltpu.VMEM((all_rows, HD), f32),
            pltpu.VMEM((block, per_group * HD), bf16),
            pltpu.SemaphoreType.DMA((5,)),
            pltpu.SemaphoreType.DMA,
            pltpu.SemaphoreType.DMA((2,)),
            pltpu.SemaphoreType.DMA,
            pltpu.SemaphoreType.DMA,
            pltpu.SemaphoreType.DMA((3,)),
            pltpu.SemaphoreType.DMA((n_ctx, 2)),
            pltpu.SemaphoreType.DMA,
            pltpu.SemaphoreType.DMA,
        ],
        compiler_params=pltpu.CompilerParams(
            collective_id=0, has_side_effects=True, vmem_limit_bytes=60 * 2**20
        ),
        cost_estimate=pl.CostEstimate(
            flops=4 * all_rows * 2 * keys * HD,
            bytes_accessed=2**22,
            transcendentals=all_rows * 2 * keys,
        ),
        name="attend",
    )(
        clip_order,
        key_counts,
        tile_mask,
        queries,
        noisy_keys,
        noisy_values,
        clean_keys,
        clean_values,
    )


def solution(mesh):
    split = P("section", ("ctx", "head"), None)
    return jax.shard_map(
        local,
        mesh=mesh,
        in_specs=(split,) * 5 + (P(),) * 3,
        out_specs=split,
        check_vma=False,
    )
```

```python
import functools
import math

import jax
import jax.numpy as jnp
from jax import lax
from jax.experimental import pallas as pl
from jax.experimental.pallas import tpu as pltpu
from jax.sharding import PartitionSpec as P

MESH = pl.DeviceIdType.MESH
HD = 128
TILE = 128
CLOSED = -1e30
EXP_SCALE = math.log2(math.e) * HD ** -0.5


def remote(src, dst, send_sem, recv_sem, device):
    return pltpu.make_async_remote_copy(
        src_ref=src,
        dst_ref=dst,
        send_sem=send_sem,
        recv_sem=recv_sem,
        device_id=device,
        device_id_type=MESH,
    )


def kernel(
    dims,
    order_hbm,
    counts_hbm,
    mask_hbm,
    q_ref,
    nk_ref,
    nv_ref,
    ck_ref,
    cv_ref,
    out_ref,
    order_ref,
    counts_ref,
    mask_ref,
    stage_kv,
    stage_q,
    qbuf,
    qcat,
    kv,
    kx,
    acc,
    run_max,
    score_a,
    score_b,
    max_a,
    max_b,
    obuf,
    load_sem,
    kv_send,
    kv_recv,
    q_send,
    q_recv,
    ring_send,
    ring_recv,
    out_send,
    out_recv,
):
    n_ctx, n_head, rows, per_group = dims
    chips = n_ctx // 2
    half = chips // 2
    block = rows * n_head
    pair_keys = 2 * block
    q_cols = per_group * HD
    tiles = block // TILE
    s = lax.axis_index("section")
    c = lax.axis_index("ctx")
    h = lax.axis_index("head")
    other = 1 - s
    z = c // 2
    core = c % 2
    sib = (s, 2 * z + 1 - core, h)
    up = (s, lax.rem(c + 2, n_ctx), h)
    down = (s, lax.rem(c + n_ctx - 2, n_ctx), h)

    def peer(d):
        return lax.rem(h + d, n_head)

    def head_rows(number):
        return pl.ds(pl.multiple_of(number * rows, rows), rows)

    def head_cols(number, width):
        return pl.ds(pl.multiple_of(number * width, width), width)

    def block_rows(number):
        return pl.ds(pl.multiple_of(number * block, block), block)

    for a, ref in enumerate((nk_ref, nv_ref, ck_ref, cv_ref)):
        pltpu.make_async_copy(ref.at[0], stage_kv.at[a], load_sem.at[0]).start()
    load_q = pltpu.make_async_copy(q_ref.at[0], stage_q, load_sem.at[1])
    load_q.start()
    load_tables = [
        pltpu.make_async_copy(order_hbm, order_ref, load_sem.at[2]),
        pltpu.make_async_copy(counts_hbm, counts_ref, load_sem.at[3]),
        pltpu.make_async_copy(mask_hbm, mask_ref, load_sem.at[4]),
    ]
    for copy in load_tables:
        copy.start()

    barrier = pltpu.get_barrier_semaphore()
    greeted = [(s, c, peer(d)) for d in range(1, n_head)]
    greeted += [(other, c, peer(d)) for d in range(n_head)]
    greeted += [sib, up, down]
    for device in greeted:
        pl.semaphore_signal(barrier, inc=1, device_id=device, device_id_type=MESH)
    pltpu.make_async_copy(stage_kv, stage_kv, load_sem.at[0]).wait()
    pl.semaphore_wait(barrier, len(greeted))

    mine = pl.ds(pl.multiple_of(c * block + h * rows, rows), rows)

    def send_kv(part, d, device):
        copy = remote(
            stage_kv.at[2 * part:2 * part + 2, :, head_cols(peer(d), HD)],
            kv.at[2 * part:2 * part + 2, mine, :],
            kv_send,
            kv_recv.at[part],
            device,
        )
        copy.start()

    for d in range(1, n_head):
        send_kv(0, d, (s, c, peer(d)))
    pltpu.make_async_copy(
        stage_kv.at[0:2, :, head_cols(h, HD)], kv.at[0:2, mine, :], kv_recv.at[0]
    ).start()
    for d in range(n_head):
        send_kv(1, d, (other, c, peer(d)))

    def view(b, part):
        return kv.at[pl.ds(2 * part, 2), block_rows(b), :]

    def arrived(b, part):
        pltpu.make_async_copy(view(b, part), view(b, part), ring_recv.at[b, part]).wait()

    def ring_block(i, way):
        if way == "up":
            return lax.rem(c + n_ctx - 2 * i, n_ctx)
        return lax.rem(c + 2 * i, n_ctx)

    plans = {}
    for i in range(half + 1):
        for part in range(2):
            for number, (way, device) in enumerate((("up", up), ("down", down))):
                if i < half:
                    plans[way, i, part] = number, device
                if 0 < i < half or way == "up":
                    plans["sib", way, i, part] = 2, sib

    def copy_of(*name):
        number, device = plans[name]
        way, i, part = name[-3:]
        b = ring_block(i, way)
        piece = view(b, part)
        if name[0] != "sib" and i == half - 1:
            piece = piece.at[0:1] if way == "up" else piece.at[1:2]
        return remote(piece, piece, ring_send.at[number], ring_recv.at[b, part], device)

    def spread(i, way, part):
        for name in ((way, i, part), ("sib", way, i, part)):
            if name in plans:
                copy_of(*name).start()

    def from_ring(i, part):
        for way in ("up", "down"):
            if ("sib", way, i, part) in plans:
                arrived(ring_block(i, way), part)
                spread(i, way, part)

    def from_sib(delta, part):
        chip = lax.rem(z + delta + chips, chips)
        arrived(2 * chip + 1 - core, part)

    for part in range(2):
        if part == 1:
            load_q.wait()
            q_mine = head_rows(h)
            for d in range(1, n_head):
                copy = remote(
                    stage_q.at[:, head_cols(peer(d), q_cols)],
                    qbuf.at[q_mine, :],
                    q_send,
                    q_recv,
                    (s, c, peer(d)),
                )
                copy.start()
            pltpu.make_async_copy(
                stage_q.at[:, head_cols(h, q_cols)], qbuf.at[q_mine, :], q_recv
            ).start()
        both = kv.at[2 * part:2 * part + 2, block_rows(c), :]
        pltpu.make_async_copy(both, both, kv_recv.at[part]).wait()
        spread(0, "down", part)
        spread(0, "up", part)

    lane = lax.broadcasted_iota(jnp.int32, (TILE, HD), 1)
    row = lax.broadcasted_iota(jnp.int32, (TILE, HD), 0)
    for head in range(per_group):
        for t in range(tiles):
            first = head * block + t * TILE
            qcat[first:first + TILE, HD:] = jnp.where(lane == t, 1.0, 0.0).astype(jnp.bfloat16)
    acc[...] = jnp.zeros_like(acc)
    run_max[...] = jnp.full_like(run_max, CLOSED)
    for copy in load_tables:
        copy.wait()
    far_order = jnp.full((TILE, HD), order_ref[other], jnp.int32)
    own_order = jnp.full((TILE, HD), order_ref[s], jnp.int32)
    earlier = jnp.where(far_order < own_order, 1, 0)

    def mask_tile(k, _):
        at = pl.ds(pl.multiple_of(k * TILE, TILE), TILE)
        seen = jnp.zeros((TILE, HD), jnp.int32)
        for t in range(tiles):
            seen = jnp.where(lane == t, mask_ref[s, tiles * c + t, k], seen)
        limit = jnp.where(seen > 0, counts_ref[s, k], 0)
        kx[0, at, :] = jnp.where((lane < tiles) & (row >= limit), CLOSED, 0.0).astype(jnp.bfloat16)
        limit = earlier * counts_ref[other, k]
        kx[1, at, :] = jnp.where((lane < tiles) & (row >= limit), CLOSED, 0.0).astype(jnp.bfloat16)
        return 0

    lax.fori_loop(0, n_ctx * tiles, mask_tile, 0)

    from_ring(1, 0)
    pltpu.make_async_copy(qbuf, qbuf, q_recv).wait()
    for head in range(per_group):
        qcat[head * block:(head + 1) * block, :HD] = qbuf[:, head * HD:(head + 1) * HD]
    from_sib(0, 0)

    def chunk(n):
        i, r = (n + 2) // 4, (n + 2) % 4
        alone = (half - i % half) // half
        part = (1 - alone) * (r // 2) + alone * (r % 2)
        chip = lax.rem(z + chips + i * (2 * (r % 2) - 1), chips)
        return part, pl.ds(pl.multiple_of(chip * pair_keys, pair_keys), pair_keys)

    def scores(where, score_ref, max_ref):
        part, at = where
        keys = jnp.concatenate([kv[2 * part, at, :], kx[part, at, :]], 1)
        found = lax.dot_general(
            qcat[...], keys, (((1,), (1,)), ((), ())), preferred_element_type=jnp.float32
        )
        score_ref[...] = found
        top = found[:, :HD]
        for t in range(1, pair_keys // HD):
            top = jnp.maximum(top, found[:, t * HD:(t + 1) * HD])
        max_ref[...] = top

    def fold(where, score_ref, max_ref):
        part, at = where
        old = run_max[...]
        new = jnp.maximum(old, jnp.max(max_ref[...], axis=1, keepdims=True))
        factor = jnp.exp2((old - new) * EXP_SCALE)
        run_max[...] = new
        pieces = []
        for t in range(pair_keys // HD):
            piece = score_ref[:, t * HD:(t + 1) * HD]
            pieces.append(jnp.exp2((piece - new) * EXP_SCALE).astype(jnp.bfloat16))
        weights = jnp.concatenate(pieces, 1)
        ones = jnp.ones((pair_keys, HD), jnp.bfloat16)
        values = jnp.concatenate([kv[2 * part + 1, at, :], ones], 1)
        added = jnp.dot(weights, values, preferred_element_type=jnp.float32)
        acc[...] = acc[...] * jnp.concatenate([factor, factor], 1) + added

    todo = {n: [] for n in range(1, 4 * half)}
    todo[1] += [functools.partial(from_sib, 0, 1)]
    for i in range(1, half + 1):
        first = 4 * i - 2
        for part in range(2):
            if i < half:
                todo[first + 2 * part] += [functools.partial(from_sib, -i, part)]
                todo[first + 2 * part + 1] += [functools.partial(from_sib, i, part)]
            else:
                todo[first + part] += [functools.partial(from_sib, i, part)]
    ring_at = {2: [(1, 1)], 4: [(2, 0)], 6: [(2, 1)], 8: [(3, 0)], 10: [(3, 1)], 11: [(4, 0)], 13: [(4, 1)]}
    for n, events in ring_at.items():
        todo[n] = [functools.partial(from_ring, *event) for event in events] + todo[n]
    scores(chunk(0), score_a, max_a)

    def prepare(k, odd):
        for n, actions in todo.items():
            if n % 2 == odd and n < 4 * half - 1:

                @pl.when(k == (n - odd) // 2)
                def _(actions=actions):
                    for action in actions:
                        action()

    def step(k, _):
        prepare(k, 1)
        scores(chunk(2 * k + 1), score_b, max_b)
        fold(chunk(2 * k), score_a, max_a)
        prepare(k + 1, 0)
        scores(chunk(2 * k + 2), score_a, max_a)
        fold(chunk(2 * k + 1), score_b, max_b)
        return 0

    lax.fori_loop(0, 2 * half - 1, step, 0)
    for action in todo[4 * half - 1]:
        action()
    scores(chunk(4 * half - 1), score_b, max_b)
    fold(chunk(4 * half - 2), score_a, max_a)
    fold(chunk(4 * half - 1), score_b, max_b)

    out_cols = head_cols(h, q_cols)

    def finish(there):
        for head in range(per_group):
            at = pl.ds(pl.multiple_of(head * block + there * rows, rows), rows)
            total = acc[at, :]
            obuf[head_rows(there), head * HD:(head + 1) * HD] = (
                total[:, :HD] / total[:, HD:]
            ).astype(jnp.bfloat16)

    for d in range(1, n_head):
        there = peer(d)
        finish(there)
        copy = remote(
            obuf.at[head_rows(there), :],
            out_ref.at[0, :, out_cols],
            out_send,
            out_recv,
            (s, c, there),
        )
        copy.start()
    finish(h)
    pltpu.make_async_copy(obuf.at[head_rows(h), :], out_ref.at[0, :, out_cols], out_recv).start()

    def drained(view, sem):
        pltpu.make_async_copy(view, view, sem).wait()

    away = block - rows
    drained(kv.at[0:2, 0:2 * block - rows, :], kv_send)
    drained(qbuf.at[0:away, :], q_send)
    along = kv.at[:, 0:(2 * half - 1) * block // 2, :]
    drained(along, ring_send.at[0])
    drained(along, ring_send.at[1])
    drained(kv.at[:, 0:chips * block, :], ring_send.at[2])
    drained(obuf.at[0:away, :], out_send)
    pltpu.make_async_copy(out_ref, out_ref, out_recv).wait()


def local(
    queries, noisy_keys, noisy_values, clean_keys, clean_values, clip_order, key_counts, tile_mask
):
    n_ctx = lax.axis_size("ctx")
    n_head = lax.axis_size("head")
    rows = queries.shape[1]
    groups = noisy_keys.shape[2] // HD
    heads = queries.shape[2] // HD
    per_group = heads // groups
    block = rows * n_head
    keys = block * n_ctx
    half = n_ctx // 4
    bf16, f32 = jnp.bfloat16, jnp.float32
    all_rows = per_group * block
    anywhere = pl.BlockSpec(memory_space=pl.ANY)
    return pl.pallas_call(
        functools.partial(kernel, (n_ctx, n_head, rows, per_group)),
        out_shape=pltpu.VMEM(queries.shape, queries.dtype),
        in_specs=[anywhere] * 8,
        out_specs=anywhere,
        scratch_shapes=[
            pltpu.SMEM(clip_order.shape, jnp.int32),
            pltpu.SMEM(key_counts.shape, jnp.int32),
            pltpu.SMEM(tile_mask.shape, jnp.int32),
            pltpu.VMEM((4, rows, groups * HD), bf16),
            pltpu.VMEM((rows, heads * HD), bf16),
            pltpu.VMEM((block, per_group * HD), bf16),
            pltpu.VMEM((all_rows, 2 * HD), bf16),
            pltpu.VMEM((4, keys, HD), bf16),
            pltpu.VMEM((2, keys, HD), bf16),
            pltpu.VMEM((all_rows, 2 * HD), f32),
            pltpu.VMEM((all_rows, HD), f32),
            pltpu.VMEM((all_rows, 2 * block), f32),
            pltpu.VMEM((all_rows, 2 * block), f32),
            pltpu.VMEM((all_rows, HD), f32),
            pltpu.VMEM((all_rows, HD), f32),
            pltpu.VMEM((block, per_group * HD), bf16),
            pltpu.SemaphoreType.DMA((5,)),
            pltpu.SemaphoreType.DMA,
            pltpu.SemaphoreType.DMA((2,)),
            pltpu.SemaphoreType.DMA,
            pltpu.SemaphoreType.DMA,
            pltpu.SemaphoreType.DMA((3,)),
            pltpu.SemaphoreType.DMA((n_ctx, 2)),
            pltpu.SemaphoreType.DMA,
            pltpu.SemaphoreType.DMA,
        ],
        compiler_params=pltpu.CompilerParams(
            collective_id=0, has_side_effects=True, vmem_limit_bytes=60 * 2**20
        ),
        cost_estimate=pl.CostEstimate(
            flops=4 * all_rows * 2 * keys * HD,
            bytes_accessed=2**22,
            transcendentals=all_rows * 2 * keys,
        ),
        name="attend",
    )(
        clip_order,
        key_counts,
        tile_mask,
        queries,
        noisy_keys,
        noisy_values,
        clean_keys,
        clean_values,
    )


def solution(mesh):
    split = P("section", ("ctx", "head"), None)
    return jax.shard_map(
        local,
        mesh=mesh,
        in_specs=(split,) * 5 + (P(),) * 3,
        out_specs=split,
        check_vma=False,
    )
```

```python
import functools
import math

import jax
import jax.numpy as jnp
from jax import lax
from jax.experimental import pallas as pl
from jax.experimental.pallas import tpu as pltpu
from jax.sharding import PartitionSpec as P

MESH = pl.DeviceIdType.MESH
HD = 128
TILE = 128
CLOSED = -1e30
EXP_SCALE = math.log2(math.e) * HD ** -0.5


def remote(src, dst, send_sem, recv_sem, device):
    return pltpu.make_async_remote_copy(
        src_ref=src,
        dst_ref=dst,
        send_sem=send_sem,
        recv_sem=recv_sem,
        device_id=device,
        device_id_type=MESH,
    )


def kernel(
    dims,
    order_hbm,
    counts_hbm,
    mask_hbm,
    q_ref,
    nk_ref,
    nv_ref,
    ck_ref,
    cv_ref,
    out_ref,
    order_ref,
    counts_ref,
    mask_ref,
    stage_kv,
    stage_q,
    qbuf,
    qcat,
    kv,
    kx,
    acc,
    run_max,
    score_a,
    score_b,
    max_a,
    max_b,
    obuf,
    load_sem,
    kv_send,
    kv_recv,
    q_send,
    q_recv,
    ring_send,
    ring_recv,
    out_send,
    out_recv,
):
    n_ctx, n_head, rows, per_group = dims
    chips = n_ctx // 2
    half = chips // 2
    block = rows * n_head
    pair_keys = 2 * block
    q_cols = per_group * HD
    tiles = block // TILE
    s = lax.axis_index("section")
    c = lax.axis_index("ctx")
    h = lax.axis_index("head")
    other = 1 - s
    z = c // 2
    core = c % 2
    sib = (s, 2 * z + 1 - core, h)
    up = (s, lax.rem(c + 2, n_ctx), h)
    down = (s, lax.rem(c + n_ctx - 2, n_ctx), h)

    def peer(d):
        return lax.rem(h + d, n_head)

    def head_rows(number):
        return pl.ds(pl.multiple_of(number * rows, rows), rows)

    def head_cols(number, width):
        return pl.ds(pl.multiple_of(number * width, width), width)

    def block_rows(number):
        return pl.ds(pl.multiple_of(number * block, block), block)

    for a, ref in enumerate((nk_ref, nv_ref, ck_ref, cv_ref)):
        pltpu.make_async_copy(ref.at[0], stage_kv.at[a], load_sem.at[0]).start()
    load_q = pltpu.make_async_copy(q_ref.at[0], stage_q, load_sem.at[1])
    load_q.start()
    load_tables = [
        pltpu.make_async_copy(order_hbm, order_ref, load_sem.at[2]),
        pltpu.make_async_copy(counts_hbm, counts_ref, load_sem.at[3]),
        pltpu.make_async_copy(mask_hbm, mask_ref, load_sem.at[4]),
    ]
    for copy in load_tables:
        copy.start()

    barrier = pltpu.get_barrier_semaphore()
    greeted = [(s, c, peer(d)) for d in range(1, n_head)]
    greeted += [(other, c, peer(d)) for d in range(n_head)]
    greeted += [sib, up, down]
    for device in greeted:
        pl.semaphore_signal(barrier, inc=1, device_id=device, device_id_type=MESH)
    pltpu.make_async_copy(stage_kv, stage_kv, load_sem.at[0]).wait()
    pl.semaphore_wait(barrier, len(greeted))

    mine = pl.ds(pl.multiple_of(c * block + h * rows, rows), rows)

    def send_kv(part, d, device):
        copy = remote(
            stage_kv.at[2 * part:2 * part + 2, :, head_cols(peer(d), HD)],
            kv.at[2 * part:2 * part + 2, mine, :],
            kv_send,
            kv_recv.at[part],
            device,
        )
        copy.start()

    for d in range(1, n_head):
        send_kv(0, d, (s, c, peer(d)))
    pltpu.make_async_copy(
        stage_kv.at[0:2, :, head_cols(h, HD)], kv.at[0:2, mine, :], kv_recv.at[0]
    ).start()
    for d in range(n_head):
        send_kv(1, d, (other, c, peer(d)))

    def view(b, part):
        return kv.at[pl.ds(2 * part, 2), block_rows(b), :]

    def arrived(b, part):
        pltpu.make_async_copy(view(b, part), view(b, part), ring_recv.at[b, part]).wait()

    def ring_block(i, way):
        if way == "up":
            return lax.rem(c + n_ctx - 2 * i, n_ctx)
        return lax.rem(c + 2 * i, n_ctx)

    plans = {}
    for i in range(half + 1):
        for part in range(2):
            for number, (way, device) in enumerate((("up", up), ("down", down))):
                if i < half:
                    plans[way, i, part] = number, device
                if 0 < i < half or way == "up":
                    plans["sib", way, i, part] = 2, sib

    def copy_of(*name):
        number, device = plans[name]
        way, i, part = name[-3:]
        b = ring_block(i, way)
        piece = view(b, part)
        if name[0] != "sib" and i == half - 1:
            piece = piece.at[0:1] if way == "up" else piece.at[1:2]
        return remote(piece, piece, ring_send.at[number], ring_recv.at[b, part], device)

    def spread(i, way, part):
        for name in ((way, i, part), ("sib", way, i, part)):
            if name in plans:
                copy_of(*name).start()

    def from_ring(i, part):
        for way in ("up", "down"):
            if ("sib", way, i, part) in plans:
                arrived(ring_block(i, way), part)
                spread(i, way, part)

    def from_sib(delta, part):
        chip = lax.rem(z + delta + chips, chips)
        arrived(2 * chip + 1 - core, part)

    for part in range(2):
        if part == 1:
            load_q.wait()
            q_mine = head_rows(h)
            for d in range(1, n_head):
                copy = remote(
                    stage_q.at[:, head_cols(peer(d), q_cols)],
                    qbuf.at[q_mine, :],
                    q_send,
                    q_recv,
                    (s, c, peer(d)),
                )
                copy.start()
            pltpu.make_async_copy(
                stage_q.at[:, head_cols(h, q_cols)], qbuf.at[q_mine, :], q_recv
            ).start()
        both = kv.at[2 * part:2 * part + 2, block_rows(c), :]
        pltpu.make_async_copy(both, both, kv_recv.at[part]).wait()
        spread(0, "down", part)
        spread(0, "up", part)

    lane = lax.broadcasted_iota(jnp.int32, (TILE, HD), 1)
    row = lax.broadcasted_iota(jnp.int32, (TILE, HD), 0)
    part_rows = rows // 2
    owners = n_head // tiles
    half_rows = per_group * TILE
    tile_of_row = row // (owners * part_rows)
    for first in range(0, 2 * half_rows, TILE):
        qcat[first:first + TILE, HD:] = jnp.where(lane == tile_of_row, 1.0, 0.0).astype(
            jnp.bfloat16
        )
    acc[...] = jnp.zeros_like(acc)
    run_max[...] = jnp.full_like(run_max, CLOSED)
    for copy in load_tables:
        copy.wait()
    far_order = jnp.full((TILE, HD), order_ref[other], jnp.int32)
    own_order = jnp.full((TILE, HD), order_ref[s], jnp.int32)
    earlier = jnp.where(far_order < own_order, 1, 0)

    def mask_tile(k, _):
        at = pl.ds(pl.multiple_of(k * TILE, TILE), TILE)
        seen = jnp.zeros((TILE, HD), jnp.int32)
        for t in range(tiles):
            seen = jnp.where(lane == t, mask_ref[s, tiles * c + t, k], seen)
        limit = jnp.where(seen > 0, counts_ref[s, k], 0)
        kx[0, at, :] = jnp.where((lane < tiles) & (row >= limit), CLOSED, 0.0).astype(jnp.bfloat16)
        limit = earlier * counts_ref[other, k]
        kx[1, at, :] = jnp.where((lane < tiles) & (row >= limit), CLOSED, 0.0).astype(jnp.bfloat16)
        return 0

    lax.fori_loop(0, n_ctx * tiles, mask_tile, 0)

    from_ring(1, 0)
    pltpu.make_async_copy(qbuf, qbuf, q_recv).wait()
    for side in range(2):
        for head in range(per_group):
            for owner in range(n_head):
                to = side * half_rows + head * TILE + owner * part_rows
                at = owner * rows + side * part_rows
                qcat[to:to + part_rows, :HD] = qbuf[
                    at:at + part_rows, head * HD:(head + 1) * HD
                ]
    from_sib(0, 0)

    def chunk(n):
        i, r = (n + 2) // 4, (n + 2) % 4
        alone = (half - i % half) // half
        part = (1 - alone) * (r // 2) + alone * (r % 2)
        chip = lax.rem(z + chips + i * (2 * (r % 2) - 1), chips)
        return part, pl.ds(pl.multiple_of(chip * pair_keys, pair_keys), pair_keys)

    def scores(where, score_ref, max_ref, side=slice(None)):
        part, at = where
        keys = jnp.concatenate([kv[2 * part, at, :], kx[part, at, :]], 1)
        found = lax.dot_general(
            qcat[side, :], keys, (((1,), (1,)), ((), ())), preferred_element_type=jnp.float32
        )
        score_ref[side, :] = found
        top = found[:, :HD]
        for t in range(1, pair_keys // HD):
            top = jnp.maximum(top, found[:, t * HD:(t + 1) * HD])
        max_ref[side, :] = top

    def fold(where, score_ref, max_ref, side=slice(None)):
        part, at = where
        old = run_max[side, :]
        new = jnp.maximum(old, jnp.max(max_ref[side, :], axis=1, keepdims=True))
        factor = jnp.exp2((old - new) * EXP_SCALE)
        run_max[side, :] = new
        pieces = []
        for t in range(pair_keys // HD):
            piece = score_ref[side, t * HD:(t + 1) * HD]
            pieces.append(jnp.exp2((piece - new) * EXP_SCALE).astype(jnp.bfloat16))
        weights = jnp.concatenate(pieces, 1)
        ones = jnp.ones((pair_keys, HD), jnp.bfloat16)
        values = jnp.concatenate([kv[2 * part + 1, at, :], ones], 1)
        added = jnp.dot(weights, values, preferred_element_type=jnp.float32)
        acc[side, :] = acc[side, :] * jnp.concatenate([factor, factor], 1) + added

    todo = {n: [] for n in range(1, 4 * half)}
    todo[1] += [functools.partial(from_sib, 0, 1)]
    for i in range(1, half + 1):
        first = 4 * i - 2
        for part in range(2):
            if i < half:
                todo[first + 2 * part] += [functools.partial(from_sib, -i, part)]
                todo[first + 2 * part + 1] += [functools.partial(from_sib, i, part)]
            else:
                todo[first + part] += [functools.partial(from_sib, i, part)]
    ring_at = {2: [(1, 1)], 4: [(2, 0)], 6: [(2, 1)], 8: [(3, 0)], 10: [(3, 1)], 11: [(4, 0)], 13: [(4, 1)]}
    for n, events in ring_at.items():
        todo[n] = [functools.partial(from_ring, *event) for event in events] + todo[n]
    scores(chunk(0), score_a, max_a)

    def prepare(k, odd):
        for n, actions in todo.items():
            if n % 2 == odd and n < 4 * half - 1:

                @pl.when(k == (n - odd) // 2)
                def _(actions=actions):
                    for action in actions:
                        action()

    def step(k, _):
        prepare(k, 1)
        scores(chunk(2 * k + 1), score_b, max_b)
        fold(chunk(2 * k), score_a, max_a)
        prepare(k + 1, 0)
        scores(chunk(2 * k + 2), score_a, max_a)
        fold(chunk(2 * k + 1), score_b, max_b)
        return 0

    lax.fori_loop(0, 2 * half - 1, step, 0)
    for action in todo[4 * half - 1]:
        action()

    out_cols = head_cols(h, q_cols)

    def finish(number, there):
        to = pl.ds(pl.multiple_of(there * rows + number * part_rows, part_rows), part_rows)
        for head in range(per_group):
            first = number * half_rows + head * TILE + there * part_rows
            total = acc[pl.ds(pl.multiple_of(first, part_rows), part_rows), :]
            obuf[to, head * HD:(head + 1) * HD] = (total[:, :HD] / total[:, HD:]).astype(
                jnp.bfloat16
            )
        return obuf.at[to, :], out_ref.at[0, number * part_rows:(number + 1) * part_rows, out_cols]

    for number in range(2):
        side = slice(number * half_rows, (number + 1) * half_rows)
        scores(chunk(4 * half - 1), score_b, max_b, side)
        fold(chunk(4 * half - 2), score_a, max_a, side)
        fold(chunk(4 * half - 1), score_b, max_b, side)
        for d in range(1, n_head):
            here, there = finish(number, peer(d))
            remote(here, there, out_send, out_recv, (s, c, peer(d))).start()
        here, there = finish(number, h)
        pltpu.make_async_copy(here, there, out_recv).start()

    def drained(view, sem):
        pltpu.make_async_copy(view, view, sem).wait()

    away = block - rows
    drained(kv.at[0:2, 0:2 * block - rows, :], kv_send)
    drained(qbuf.at[0:away, :], q_send)
    along = kv.at[:, 0:(2 * half - 1) * block // 2, :]
    drained(along, ring_send.at[0])
    drained(along, ring_send.at[1])
    drained(kv.at[:, 0:chips * block, :], ring_send.at[2])
    drained(obuf.at[0:away, :], out_send)
    pltpu.make_async_copy(out_ref, out_ref, out_recv).wait()


def local(
    queries, noisy_keys, noisy_values, clean_keys, clean_values, clip_order, key_counts, tile_mask
):
    n_ctx = lax.axis_size("ctx")
    n_head = lax.axis_size("head")
    rows = queries.shape[1]
    groups = noisy_keys.shape[2] // HD
    heads = queries.shape[2] // HD
    per_group = heads // groups
    block = rows * n_head
    keys = block * n_ctx
    half = n_ctx // 4
    bf16, f32 = jnp.bfloat16, jnp.float32
    all_rows = per_group * block
    anywhere = pl.BlockSpec(memory_space=pl.ANY)
    return pl.pallas_call(
        functools.partial(kernel, (n_ctx, n_head, rows, per_group)),
        out_shape=pltpu.VMEM(queries.shape, queries.dtype),
        in_specs=[anywhere] * 8,
        out_specs=anywhere,
        scratch_shapes=[
            pltpu.SMEM(clip_order.shape, jnp.int32),
            pltpu.SMEM(key_counts.shape, jnp.int32),
            pltpu.SMEM(tile_mask.shape, jnp.int32),
            pltpu.VMEM((4, rows, groups * HD), bf16),
            pltpu.VMEM((rows, heads * HD), bf16),
            pltpu.VMEM((block, per_group * HD), bf16),
            pltpu.VMEM((all_rows, 2 * HD), bf16),
            pltpu.VMEM((4, keys, HD), bf16),
            pltpu.VMEM((2, keys, HD), bf16),
            pltpu.VMEM((all_rows, 2 * HD), f32),
            pltpu.VMEM((all_rows, HD), f32),
            pltpu.VMEM((all_rows, 2 * block), f32),
            pltpu.VMEM((all_rows, 2 * block), f32),
            pltpu.VMEM((all_rows, HD), f32),
            pltpu.VMEM((all_rows, HD), f32),
            pltpu.VMEM((block, per_group * HD), bf16),
            pltpu.SemaphoreType.DMA((5,)),
            pltpu.SemaphoreType.DMA,
            pltpu.SemaphoreType.DMA((2,)),
            pltpu.SemaphoreType.DMA,
            pltpu.SemaphoreType.DMA,
            pltpu.SemaphoreType.DMA((3,)),
            pltpu.SemaphoreType.DMA((n_ctx, 2)),
            pltpu.SemaphoreType.DMA,
            pltpu.SemaphoreType.DMA,
        ],
        compiler_params=pltpu.CompilerParams(
            collective_id=0, has_side_effects=True, vmem_limit_bytes=60 * 2**20
        ),
        cost_estimate=pl.CostEstimate(
            flops=4 * all_rows * 2 * keys * HD,
            bytes_accessed=2**22,
            transcendentals=all_rows * 2 * keys,
        ),
        name="attend",
    )(
        clip_order,
        key_counts,
        tile_mask,
        queries,
        noisy_keys,
        noisy_values,
        clean_keys,
        clean_values,
    )


def solution(mesh):
    split = P("section", ("ctx", "head"), None)
    return jax.shard_map(
        local,
        mesh=mesh,
        in_specs=(split,) * 5 + (P(),) * 3,
        out_specs=split,
        check_vma=False,
    )
```

```python
import functools
import math

import jax
import jax.numpy as jnp
from jax import lax
from jax.experimental import pallas as pl
from jax.experimental.pallas import tpu as pltpu
from jax.sharding import PartitionSpec as P

MESH = pl.DeviceIdType.MESH
HD = 128
TILE = 128
CLOSED = -1e30
EXP_SCALE = math.log2(math.e) * HD ** -0.5


def remote(src, dst, send_sem, recv_sem, device):
    return pltpu.make_async_remote_copy(
        src_ref=src,
        dst_ref=dst,
        send_sem=send_sem,
        recv_sem=recv_sem,
        device_id=device,
        device_id_type=MESH,
    )


def kernel(
    dims,
    order_hbm,
    counts_hbm,
    mask_hbm,
    q_ref,
    nk_ref,
    nv_ref,
    ck_ref,
    cv_ref,
    out_ref,
    order_ref,
    counts_ref,
    mask_ref,
    stage_kv,
    stage_q,
    qbuf,
    qcat,
    kv,
    kx,
    acc,
    run_max,
    score_a,
    score_b,
    max_a,
    max_b,
    obuf,
    load_sem,
    kv_send,
    kv_recv,
    q_send,
    q_recv,
    ring_send,
    ring_recv,
    out_send,
    out_recv,
):
    n_ctx, n_head, rows, per_group = dims
    chips = n_ctx // 2
    half = chips // 2
    block = rows * n_head
    pair_keys = 2 * block
    q_cols = per_group * HD
    tiles = block // TILE
    s = lax.axis_index("section")
    c = lax.axis_index("ctx")
    h = lax.axis_index("head")
    other = 1 - s
    z = c // 2
    core = c % 2
    sib = (s, 2 * z + 1 - core, h)
    up = (s, lax.rem(c + 2, n_ctx), h)
    down = (s, lax.rem(c + n_ctx - 2, n_ctx), h)

    def peer(d):
        return lax.rem(h + d, n_head)

    def head_rows(number):
        return pl.ds(pl.multiple_of(number * rows, rows), rows)

    def head_cols(number, width):
        return pl.ds(pl.multiple_of(number * width, width), width)

    def block_rows(number):
        return pl.ds(pl.multiple_of(number * block, block), block)

    for a, ref in enumerate((nk_ref, nv_ref, ck_ref, cv_ref)):
        pltpu.make_async_copy(ref.at[0], stage_kv.at[a], load_sem.at[0]).start()
    barrier = pltpu.get_barrier_semaphore()
    greeted = [(s, c, peer(d)) for d in range(1, n_head)]
    greeted += [(other, c, peer(d)) for d in range(n_head)]
    greeted += [sib, up, down]
    for device in greeted:
        pl.semaphore_signal(barrier, inc=1, device_id=device, device_id_type=MESH)
    load_q = pltpu.make_async_copy(q_ref.at[0], stage_q, load_sem.at[1])
    load_q.start()
    load_tables = [
        pltpu.make_async_copy(order_hbm, order_ref, load_sem.at[2]),
        pltpu.make_async_copy(counts_hbm, counts_ref, load_sem.at[3]),
        pltpu.make_async_copy(mask_hbm, mask_ref, load_sem.at[4]),
    ]
    for copy in load_tables:
        copy.start()
    pltpu.make_async_copy(stage_kv, stage_kv, load_sem.at[0]).wait()
    pl.semaphore_wait(barrier, len(greeted))

    mine = pl.ds(pl.multiple_of(c * block + h * rows, rows), rows)

    def send_kv(part, d, device):
        copy = remote(
            stage_kv.at[2 * part:2 * part + 2, :, head_cols(peer(d), HD)],
            kv.at[2 * part:2 * part + 2, mine, :],
            kv_send,
            kv_recv.at[part],
            device,
        )
        copy.start()

    for d in range(1, n_head):
        send_kv(0, d, (s, c, peer(d)))
    pltpu.make_async_copy(
        stage_kv.at[0:2, :, head_cols(h, HD)], kv.at[0:2, mine, :], kv_recv.at[0]
    ).start()
    for d in range(n_head):
        send_kv(1, d, (other, c, peer(d)))

    lane = lax.broadcasted_iota(jnp.int32, (TILE, HD), 1)
    row = lax.broadcasted_iota(jnp.int32, (TILE, HD), 0)
    part_rows = rows // 2
    owners = n_head // tiles
    half_rows = per_group * TILE
    tile_of_row = row // (owners * part_rows)
    for first in range(0, 2 * half_rows, TILE):
        qcat[first:first + TILE, HD:] = jnp.where(lane == tile_of_row, 1.0, 0.0).astype(
            jnp.bfloat16
        )
    acc[...] = jnp.zeros_like(acc)
    run_max[...] = jnp.full_like(run_max, CLOSED)
    for copy in load_tables:
        copy.wait()
    far_order = jnp.full((TILE, HD), order_ref[other], jnp.int32)
    own_order = jnp.full((TILE, HD), order_ref[s], jnp.int32)
    earlier = jnp.where(far_order < own_order, 1, 0)

    def mask_tile(k, _):
        at = pl.ds(pl.multiple_of(k * TILE, TILE), TILE)
        seen = jnp.zeros((TILE, HD), jnp.int32)
        for t in range(tiles):
            seen = jnp.where(lane == t, mask_ref[s, tiles * c + t, k], seen)
        limit = jnp.where(seen > 0, counts_ref[s, k], 0)
        kx[0, at, :] = jnp.where((lane < tiles) & (row >= limit), CLOSED, 0.0).astype(jnp.bfloat16)
        limit = earlier * counts_ref[other, k]
        kx[1, at, :] = jnp.where((lane < tiles) & (row >= limit), CLOSED, 0.0).astype(jnp.bfloat16)
        return 0

    lax.fori_loop(0, n_ctx * tiles, mask_tile, 0)

    def view(b, part):
        return kv.at[pl.ds(2 * part, 2), block_rows(b), :]

    def arrived(b, part):
        pltpu.make_async_copy(view(b, part), view(b, part), ring_recv.at[b, part]).wait()

    def ring_block(i, way):
        if way == "up":
            return lax.rem(c + n_ctx - 2 * i, n_ctx)
        return lax.rem(c + 2 * i, n_ctx)

    plans = {}
    for i in range(half + 1):
        for part in range(2):
            for number, (way, device) in enumerate((("up", up), ("down", down))):
                if i < half:
                    plans[way, i, part] = number, device
                if 0 < i < half or way == "up":
                    plans["sib", way, i, part] = 2, sib

    def copy_of(*name):
        number, device = plans[name]
        way, i, part = name[-3:]
        b = ring_block(i, way)
        piece = view(b, part)
        if name[0] != "sib" and i == half - 1:
            piece = piece.at[0:1] if way == "up" else piece.at[1:2]
        return remote(piece, piece, ring_send.at[number], ring_recv.at[b, part], device)

    def spread(i, way, part):
        for name in ((way, i, part), ("sib", way, i, part)):
            if name in plans:
                copy_of(*name).start()

    def from_ring(i, part):
        for way in ("up", "down"):
            if ("sib", way, i, part) in plans:
                arrived(ring_block(i, way), part)
                spread(i, way, part)

    def from_sib(delta, part):
        chip = lax.rem(z + delta + chips, chips)
        arrived(2 * chip + 1 - core, part)

    for part in range(2):
        if part == 1:
            load_q.wait()
            q_mine = head_rows(h)
            for d in range(1, n_head):
                copy = remote(
                    stage_q.at[:, head_cols(peer(d), q_cols)],
                    qbuf.at[q_mine, :],
                    q_send,
                    q_recv,
                    (s, c, peer(d)),
                )
                copy.start()
            pltpu.make_async_copy(
                stage_q.at[:, head_cols(h, q_cols)], qbuf.at[q_mine, :], q_recv
            ).start()
        both = kv.at[2 * part:2 * part + 2, block_rows(c), :]
        pltpu.make_async_copy(both, both, kv_recv.at[part]).wait()
        spread(0, "down", part)
        spread(0, "up", part)

    from_ring(1, 0)
    pltpu.make_async_copy(qbuf, qbuf, q_recv).wait()
    for side in range(2):
        for head in range(per_group):
            for owner in range(n_head):
                to = side * half_rows + head * TILE + owner * part_rows
                at = owner * rows + side * part_rows
                qcat[to:to + part_rows, :HD] = qbuf[
                    at:at + part_rows, head * HD:(head + 1) * HD
                ]
    from_sib(0, 0)

    def chunk(n):
        i, r = (n + 2) // 4, (n + 2) % 4
        alone = (half - i % half) // half
        part = (1 - alone) * (r // 2) + alone * (r % 2)
        chip = lax.rem(z + chips + i * (2 * (r % 2) - 1), chips)
        return part, pl.ds(pl.multiple_of(chip * pair_keys, pair_keys), pair_keys)

    def scores(where, score_ref, max_ref, side=slice(None)):
        part, at = where
        keys = jnp.concatenate([kv[2 * part, at, :], kx[part, at, :]], 1)
        found = lax.dot_general(
            qcat[side, :], keys, (((1,), (1,)), ((), ())), preferred_element_type=jnp.float32
        )
        score_ref[side, :] = found
        top = found[:, :HD]
        for t in range(1, pair_keys // HD):
            top = jnp.maximum(top, found[:, t * HD:(t + 1) * HD])
        max_ref[side, :] = top

    def fold(where, score_ref, max_ref, side=slice(None)):
        part, at = where
        old = run_max[side, :]
        new = jnp.maximum(old, jnp.max(max_ref[side, :], axis=1, keepdims=True))
        factor = jnp.exp2((old - new) * EXP_SCALE)
        run_max[side, :] = new
        pieces = []
        for t in range(pair_keys // HD):
            piece = score_ref[side, t * HD:(t + 1) * HD]
            pieces.append(jnp.exp2((piece - new) * EXP_SCALE).astype(jnp.bfloat16))
        weights = jnp.concatenate(pieces, 1)
        ones = jnp.ones((pair_keys, HD), jnp.bfloat16)
        values = jnp.concatenate([kv[2 * part + 1, at, :], ones], 1)
        added = jnp.dot(weights, values, preferred_element_type=jnp.float32)
        acc[side, :] = acc[side, :] * jnp.concatenate([factor, factor], 1) + added

    todo = {n: [] for n in range(1, 4 * half)}
    todo[1] += [functools.partial(from_sib, 0, 1)]
    for i in range(1, half + 1):
        first = 4 * i - 2
        for part in range(2):
            if i < half:
                todo[first + 2 * part] += [functools.partial(from_sib, -i, part)]
                todo[first + 2 * part + 1] += [functools.partial(from_sib, i, part)]
            else:
                todo[first + part] += [functools.partial(from_sib, i, part)]
    ring_at = {2: [(1, 1)], 4: [(2, 0)], 6: [(2, 1)], 8: [(3, 0)], 10: [(3, 1)], 11: [(4, 0)], 13: [(4, 1)]}
    for n, events in ring_at.items():
        todo[n] = [functools.partial(from_ring, *event) for event in events] + todo[n]
    scores(chunk(0), score_a, max_a)

    def prepare(k, odd):
        for n, actions in todo.items():
            if n % 2 == odd and n < 4 * half - 1:

                @pl.when(k == (n - odd) // 2)
                def _(actions=actions):
                    for action in actions:
                        action()

    def step(k, _):
        prepare(k, 1)
        scores(chunk(2 * k + 1), score_b, max_b)
        fold(chunk(2 * k), score_a, max_a)
        prepare(k + 1, 0)
        scores(chunk(2 * k + 2), score_a, max_a)
        fold(chunk(2 * k + 1), score_b, max_b)
        return 0

    lax.fori_loop(0, 2 * half - 1, step, 0)
    for action in todo[4 * half - 1]:
        action()

    out_cols = head_cols(h, q_cols)

    def finish(number, there):
        to = pl.ds(pl.multiple_of(there * rows + number * part_rows, part_rows), part_rows)
        for head in range(per_group):
            first = number * half_rows + head * TILE + there * part_rows
            total = acc[pl.ds(pl.multiple_of(first, part_rows), part_rows), :]
            obuf[to, head * HD:(head + 1) * HD] = (total[:, :HD] / total[:, HD:]).astype(
                jnp.bfloat16
            )
        return obuf.at[to, :], out_ref.at[0, number * part_rows:(number + 1) * part_rows, out_cols]

    for number in range(2):
        side = slice(number * half_rows, (number + 1) * half_rows)
        scores(chunk(4 * half - 1), score_b, max_b, side)
        fold(chunk(4 * half - 2), score_a, max_a, side)
        fold(chunk(4 * half - 1), score_b, max_b, side)
        for d in range(1, n_head):
            here, there = finish(number, peer(d))
            remote(here, there, out_send, out_recv, (s, c, peer(d))).start()
        here, there = finish(number, h)
        pltpu.make_async_copy(here, there, out_recv).start()

    def drained(view, sem):
        pltpu.make_async_copy(view, view, sem).wait()

    away = block - rows
    drained(kv.at[0:2, 0:2 * block - rows, :], kv_send)
    drained(qbuf.at[0:away, :], q_send)
    along = kv.at[:, 0:(2 * half - 1) * block // 2, :]
    drained(along, ring_send.at[0])
    drained(along, ring_send.at[1])
    drained(kv.at[:, 0:chips * block, :], ring_send.at[2])
    drained(obuf.at[0:away, :], out_send)
    pltpu.make_async_copy(out_ref, out_ref, out_recv).wait()


def local(
    queries, noisy_keys, noisy_values, clean_keys, clean_values, clip_order, key_counts, tile_mask
):
    n_ctx = lax.axis_size("ctx")
    n_head = lax.axis_size("head")
    rows = queries.shape[1]
    groups = noisy_keys.shape[2] // HD
    heads = queries.shape[2] // HD
    per_group = heads // groups
    block = rows * n_head
    keys = block * n_ctx
    half = n_ctx // 4
    bf16, f32 = jnp.bfloat16, jnp.float32
    all_rows = per_group * block
    anywhere = pl.BlockSpec(memory_space=pl.ANY)
    return pl.pallas_call(
        functools.partial(kernel, (n_ctx, n_head, rows, per_group)),
        out_shape=pltpu.VMEM(queries.shape, queries.dtype),
        in_specs=[anywhere] * 8,
        out_specs=anywhere,
        scratch_shapes=[
            pltpu.SMEM(clip_order.shape, jnp.int32),
            pltpu.SMEM(key_counts.shape, jnp.int32),
            pltpu.SMEM(tile_mask.shape, jnp.int32),
            pltpu.VMEM((4, rows, groups * HD), bf16),
            pltpu.VMEM((rows, heads * HD), bf16),
            pltpu.VMEM((block, per_group * HD), bf16),
            pltpu.VMEM((all_rows, 2 * HD), bf16),
            pltpu.VMEM((4, keys, HD), bf16),
            pltpu.VMEM((2, keys, HD), bf16),
            pltpu.VMEM((all_rows, 2 * HD), f32),
            pltpu.VMEM((all_rows, HD), f32),
            pltpu.VMEM((all_rows, 2 * block), f32),
            pltpu.VMEM((all_rows, 2 * block), f32),
            pltpu.VMEM((all_rows, HD), f32),
            pltpu.VMEM((all_rows, HD), f32),
            pltpu.VMEM((block, per_group * HD), bf16),
            pltpu.SemaphoreType.DMA((5,)),
            pltpu.SemaphoreType.DMA,
            pltpu.SemaphoreType.DMA((2,)),
            pltpu.SemaphoreType.DMA,
            pltpu.SemaphoreType.DMA,
            pltpu.SemaphoreType.DMA((3,)),
            pltpu.SemaphoreType.DMA((n_ctx, 2)),
            pltpu.SemaphoreType.DMA,
            pltpu.SemaphoreType.DMA,
        ],
        compiler_params=pltpu.CompilerParams(
            collective_id=0, has_side_effects=True, vmem_limit_bytes=60 * 2**20
        ),
        cost_estimate=pl.CostEstimate(
            flops=4 * all_rows * 2 * keys * HD,
            bytes_accessed=2**22,
            transcendentals=all_rows * 2 * keys,
        ),
        name="attend",
    )(
        clip_order,
        key_counts,
        tile_mask,
        queries,
        noisy_keys,
        noisy_values,
        clean_keys,
        clean_values,
    )


def solution(mesh):
    split = P("section", ("ctx", "head"), None)
    return jax.shard_map(
        local,
        mesh=mesh,
        in_specs=(split,) * 5 + (P(),) * 3,
        out_specs=split,
        check_vma=False,
    )
```

```python
import functools
import math

import jax
import jax.numpy as jnp
from jax import lax
from jax.experimental import pallas as pl
from jax.experimental.pallas import tpu as pltpu
from jax.sharding import PartitionSpec as P

MESH = pl.DeviceIdType.MESH
HD = 128
TILE = 128
CLOSED = -1e30
EXP_SCALE = math.log2(math.e) * HD ** -0.5


def remote(src, dst, send_sem, recv_sem, device):
    return pltpu.make_async_remote_copy(
        src_ref=src,
        dst_ref=dst,
        send_sem=send_sem,
        recv_sem=recv_sem,
        device_id=device,
        device_id_type=MESH,
    )


def kernel(
    dims,
    order_hbm,
    counts_hbm,
    mask_hbm,
    q_ref,
    nk_ref,
    nv_ref,
    ck_ref,
    cv_ref,
    out_ref,
    order_ref,
    counts_ref,
    mask_ref,
    stage_kv,
    stage_q,
    qbuf,
    qcat,
    kv,
    kx,
    acc,
    run_max,
    score_a,
    score_b,
    max_a,
    max_b,
    obuf,
    load_sem,
    kv_send,
    kv_recv,
    q_send,
    q_recv,
    ring_send,
    ring_recv,
    out_send,
    out_recv,
):
    n_ctx, n_head, rows, per_group = dims
    chips = n_ctx // 2
    half = chips // 2
    block = rows * n_head
    pair_keys = 2 * block
    q_cols = per_group * HD
    tiles = block // TILE
    s = lax.axis_index("section")
    c = lax.axis_index("ctx")
    h = lax.axis_index("head")
    other = 1 - s
    z = c // 2
    core = c % 2
    sib = (s, 2 * z + 1 - core, h)
    up = (s, lax.rem(c + 2, n_ctx), h)
    down = (s, lax.rem(c + n_ctx - 2, n_ctx), h)

    def peer(d):
        return lax.rem(h + d, n_head)

    def head_rows(number):
        return pl.ds(pl.multiple_of(number * rows, rows), rows)

    def head_cols(number, width):
        return pl.ds(pl.multiple_of(number * width, width), width)

    def block_rows(number):
        return pl.ds(pl.multiple_of(number * block, block), block)

    for a, ref in enumerate((nk_ref, nv_ref, ck_ref, cv_ref)):
        pltpu.make_async_copy(ref.at[0], stage_kv.at[a], load_sem.at[0]).start()
    barrier = pltpu.get_barrier_semaphore()
    greeted = [(s, c, peer(d)) for d in range(1, n_head)]
    greeted += [(other, c, peer(d)) for d in range(n_head)]
    greeted += [sib, up, down]
    for device in greeted:
        pl.semaphore_signal(barrier, inc=1, device_id=device, device_id_type=MESH)
    load_q = pltpu.make_async_copy(q_ref.at[0], stage_q, load_sem.at[1])
    load_q.start()
    load_tables = [
        pltpu.make_async_copy(order_hbm, order_ref, load_sem.at[2]),
        pltpu.make_async_copy(counts_hbm, counts_ref, load_sem.at[3]),
        pltpu.make_async_copy(mask_hbm, mask_ref, load_sem.at[4]),
    ]
    for copy in load_tables:
        copy.start()
    pltpu.make_async_copy(stage_kv, stage_kv, load_sem.at[0]).wait()
    pl.semaphore_wait(barrier, len(greeted))

    mine = pl.ds(pl.multiple_of(c * block + h * rows, rows), rows)

    def send_kv(part, d, device):
        copy = remote(
            stage_kv.at[2 * part:2 * part + 2, :, head_cols(peer(d), HD)],
            kv.at[2 * part:2 * part + 2, mine, :],
            kv_send,
            kv_recv.at[part],
            device,
        )
        copy.start()

    for d in range(1, n_head):
        send_kv(0, d, (s, c, peer(d)))
    pltpu.make_async_copy(
        stage_kv.at[0:2, :, head_cols(h, HD)], kv.at[0:2, mine, :], kv_recv.at[0]
    ).start()
    for d in range(n_head):
        send_kv(1, d, (other, c, peer(d)))

    lane = lax.broadcasted_iota(jnp.int32, (TILE, HD), 1)
    row = lax.broadcasted_iota(jnp.int32, (TILE, HD), 0)
    part_rows = rows // 2
    owners = n_head // tiles
    half_rows = per_group * TILE
    tile_of_row = row // (owners * part_rows)
    for first in range(0, 2 * half_rows, TILE):
        qcat[first:first + TILE, HD:] = jnp.where(lane == tile_of_row, 1.0, 0.0).astype(
            jnp.bfloat16
        )
    acc[...] = jnp.zeros_like(acc)
    run_max[...] = jnp.full_like(run_max, CLOSED)
    for copy in load_tables:
        copy.wait()
    far_order = jnp.full((TILE, HD), order_ref[other], jnp.int32)
    own_order = jnp.full((TILE, HD), order_ref[s], jnp.int32)
    earlier = jnp.where(far_order < own_order, 1, 0)

    def mask_tile(k, _):
        at = pl.ds(pl.multiple_of(k * TILE, TILE), TILE)
        seen = jnp.zeros((TILE, HD), jnp.int32)
        for t in range(tiles):
            seen = jnp.where(lane == t, mask_ref[s, tiles * c + t, k], seen)
        limit = jnp.where(seen > 0, counts_ref[s, k], 0)
        kx[0, at, :] = jnp.where((lane < tiles) & (row >= limit), CLOSED, 0.0).astype(jnp.bfloat16)
        limit = earlier * counts_ref[other, k]
        kx[1, at, :] = jnp.where((lane < tiles) & (row >= limit), CLOSED, 0.0).astype(jnp.bfloat16)
        return 0

    lax.fori_loop(0, n_ctx * tiles, mask_tile, 0)

    def view(b, part):
        return kv.at[pl.ds(2 * part, 2), block_rows(b), :]

    def arrived(b, part):
        pltpu.make_async_copy(view(b, part), view(b, part), ring_recv.at[b, part]).wait()

    def ring_block(i, way):
        if way == "up":
            return lax.rem(c + n_ctx - 2 * i, n_ctx)
        return lax.rem(c + 2 * i, n_ctx)

    plans = {}
    for i in range(half + 1):
        for part in range(2):
            for number, (way, device) in enumerate((("up", up), ("down", down))):
                if i < half:
                    plans[way, i, part] = number, device
                if 0 < i < half or way == "up":
                    plans["sib", way, i, part] = 2, sib

    def copy_of(*name):
        number, device = plans[name]
        way, i, part = name[-3:]
        b = ring_block(i, way)
        piece = view(b, part)
        if name[0] != "sib" and i == half - 1:
            piece = piece.at[0:1] if way == "up" else piece.at[1:2]
        return remote(piece, piece, ring_send.at[number], ring_recv.at[b, part], device)

    def spread(i, way, part):
        for name in ((way, i, part), ("sib", way, i, part)):
            if name in plans:
                copy_of(*name).start()

    def from_ring(i, part):
        for way in ("up", "down"):
            if ("sib", way, i, part) in plans:
                arrived(ring_block(i, way), part)
                spread(i, way, part)

    def from_sib(delta, part):
        chip = lax.rem(z + delta + chips, chips)
        arrived(2 * chip + 1 - core, part)

    for part in range(2):
        if part == 1:
            load_q.wait()
            q_mine = head_rows(h)
            for d in range(1, n_head):
                copy = remote(
                    stage_q.at[:, head_cols(peer(d), q_cols)],
                    qbuf.at[q_mine, :],
                    q_send,
                    q_recv,
                    (s, c, peer(d)),
                )
                copy.start()
            pltpu.make_async_copy(
                stage_q.at[:, head_cols(h, q_cols)], qbuf.at[q_mine, :], q_recv
            ).start()
        both = kv.at[2 * part:2 * part + 2, block_rows(c), :]
        pltpu.make_async_copy(both, both, kv_recv.at[part]).wait()
        spread(0, "down", part)
        spread(0, "up", part)

    from_ring(1, 0)
    pltpu.make_async_copy(qbuf, qbuf, q_recv).wait()
    for side in range(2):
        for head in range(per_group):
            for owner in range(n_head):
                to = side * half_rows + head * TILE + owner * part_rows
                at = owner * rows + side * part_rows
                qcat[to:to + part_rows, :HD] = qbuf[
                    at:at + part_rows, head * HD:(head + 1) * HD
                ]
    from_sib(0, 0)

    def chunk(n):
        i, r = (n + 2) // 4, (n + 2) % 4
        alone = (half - i % half) // half
        part = (1 - alone) * (r // 2) + alone * (r % 2)
        chip = lax.rem(z + chips + i * (2 * (r % 2) - 1), chips)
        return part, pl.ds(pl.multiple_of(chip * pair_keys, pair_keys), pair_keys)

    def scores(where, score_ref, max_ref, side=slice(None)):
        part, at = where
        keys = jnp.concatenate([kv[2 * part, at, :], kx[part, at, :]], 1)
        found = lax.dot_general(
            qcat[side, :], keys, (((1,), (1,)), ((), ())), preferred_element_type=jnp.float32
        )
        score_ref[side, :] = found
        top = found[:, :HD]
        for t in range(1, pair_keys // HD):
            top = jnp.maximum(top, found[:, t * HD:(t + 1) * HD])
        max_ref[side, :] = top

    def fold(where, score_ref, max_ref, side=slice(None)):
        part, at = where
        old = run_max[side, :]
        new = jnp.maximum(old, jnp.max(max_ref[side, :], axis=1, keepdims=True))
        factor = jnp.exp2((old - new) * EXP_SCALE)
        run_max[side, :] = new
        pieces = []
        for t in range(pair_keys // HD):
            piece = score_ref[side, t * HD:(t + 1) * HD]
            pieces.append(jnp.exp2((piece - new) * EXP_SCALE).astype(jnp.bfloat16))
        weights = jnp.concatenate(pieces, 1)
        ones = jnp.ones((pair_keys, HD), jnp.bfloat16)
        values = jnp.concatenate([kv[2 * part + 1, at, :], ones], 1)
        added = jnp.dot(weights, values, preferred_element_type=jnp.float32)
        acc[side, :] = acc[side, :] * jnp.concatenate([factor, factor], 1) + added

    todo = {n: [] for n in range(1, 4 * half)}
    todo[1] += [functools.partial(from_sib, 0, 1)]
    for i in range(1, half + 1):
        first = 4 * i - 2
        for part in range(2):
            if i < half:
                todo[first + 2 * part] += [functools.partial(from_sib, -i, part)]
                todo[first + 2 * part + 1] += [functools.partial(from_sib, i, part)]
            else:
                todo[first + part] += [functools.partial(from_sib, i, part)]
    ring_at = {2: [(1, 1)], 4: [(2, 0)], 6: [(2, 1)], 8: [(3, 0)], 10: [(3, 1)], 11: [(4, 0)], 13: [(4, 1)]}
    for n, events in ring_at.items():
        todo[n] = [functools.partial(from_ring, *event) for event in events] + todo[n]
    scores(chunk(0), score_a, max_a)

    def prepare(k, odd):
        for n, actions in todo.items():
            if n % 2 == odd and n < 4 * half - 1:

                @pl.when(k == (n - odd) // 2)
                def _(actions=actions):
                    for action in actions:
                        action()

    def step(k, _):
        prepare(k, 1)
        scores(chunk(2 * k + 1), score_b, max_b)
        fold(chunk(2 * k), score_a, max_a)
        prepare(k + 1, 0)
        scores(chunk(2 * k + 2), score_a, max_a)
        fold(chunk(2 * k + 1), score_b, max_b)
        return 0

    lax.fori_loop(0, 2 * half - 1, step, 0)
    for action in todo[4 * half - 1]:
        action()

    out_cols = head_cols(h, q_cols)

    def finish(number, there):
        to = pl.ds(pl.multiple_of(there * rows + number * part_rows, part_rows), part_rows)
        for head in range(per_group):
            first = number * half_rows + head * TILE + there * part_rows
            total = acc[pl.ds(pl.multiple_of(first, part_rows), part_rows), :]
            obuf[to, head * HD:(head + 1) * HD] = (total[:, :HD] / total[:, HD:]).astype(
                jnp.bfloat16
            )
        return obuf.at[to, :], out_ref.at[0, number * part_rows:(number + 1) * part_rows, out_cols]

    for number in range(2):
        side = slice(number * half_rows, (number + 1) * half_rows)
        if number == 0:
            scores(chunk(4 * half - 1), score_b, max_b, side)
        fold(chunk(4 * half - 2), score_a, max_a, side)
        if number == 0:
            later = slice(half_rows, 2 * half_rows)
            scores(chunk(4 * half - 1), score_b, max_b, later)
        fold(chunk(4 * half - 1), score_b, max_b, side)
        for d in range(1, n_head):
            here, there = finish(number, peer(d))
            remote(here, there, out_send, out_recv, (s, c, peer(d))).start()
        here, there = finish(number, h)
        pltpu.make_async_copy(here, there, out_recv).start()

    def drained(view, sem):
        pltpu.make_async_copy(view, view, sem).wait()

    away = block - rows
    drained(kv.at[0:2, 0:2 * block - rows, :], kv_send)
    drained(qbuf.at[0:away, :], q_send)
    along = kv.at[:, 0:(2 * half - 1) * block // 2, :]
    drained(along, ring_send.at[0])
    drained(along, ring_send.at[1])
    drained(kv.at[:, 0:chips * block, :], ring_send.at[2])
    drained(obuf.at[0:away, :], out_send)
    pltpu.make_async_copy(out_ref, out_ref, out_recv).wait()


def local(
    queries, noisy_keys, noisy_values, clean_keys, clean_values, clip_order, key_counts, tile_mask
):
    n_ctx = lax.axis_size("ctx")
    n_head = lax.axis_size("head")
    rows = queries.shape[1]
    groups = noisy_keys.shape[2] // HD
    heads = queries.shape[2] // HD
    per_group = heads // groups
    block = rows * n_head
    keys = block * n_ctx
    half = n_ctx // 4
    bf16, f32 = jnp.bfloat16, jnp.float32
    all_rows = per_group * block
    anywhere = pl.BlockSpec(memory_space=pl.ANY)
    return pl.pallas_call(
        functools.partial(kernel, (n_ctx, n_head, rows, per_group)),
        out_shape=pltpu.VMEM(queries.shape, queries.dtype),
        in_specs=[anywhere] * 8,
        out_specs=anywhere,
        scratch_shapes=[
            pltpu.SMEM(clip_order.shape, jnp.int32),
            pltpu.SMEM(key_counts.shape, jnp.int32),
            pltpu.SMEM(tile_mask.shape, jnp.int32),
            pltpu.VMEM((4, rows, groups * HD), bf16),
            pltpu.VMEM((rows, heads * HD), bf16),
            pltpu.VMEM((block, per_group * HD), bf16),
            pltpu.VMEM((all_rows, 2 * HD), bf16),
            pltpu.VMEM((4, keys, HD), bf16),
            pltpu.VMEM((2, keys, HD), bf16),
            pltpu.VMEM((all_rows, 2 * HD), f32),
            pltpu.VMEM((all_rows, HD), f32),
            pltpu.VMEM((all_rows, 2 * block), f32),
            pltpu.VMEM((all_rows, 2 * block), f32),
            pltpu.VMEM((all_rows, HD), f32),
            pltpu.VMEM((all_rows, HD), f32),
            pltpu.VMEM((block, per_group * HD), bf16),
            pltpu.SemaphoreType.DMA((5,)),
            pltpu.SemaphoreType.DMA,
            pltpu.SemaphoreType.DMA((2,)),
            pltpu.SemaphoreType.DMA,
            pltpu.SemaphoreType.DMA,
            pltpu.SemaphoreType.DMA((3,)),
            pltpu.SemaphoreType.DMA((n_ctx, 2)),
            pltpu.SemaphoreType.DMA,
            pltpu.SemaphoreType.DMA,
        ],
        compiler_params=pltpu.CompilerParams(
            collective_id=0, has_side_effects=True, vmem_limit_bytes=60 * 2**20
        ),
        cost_estimate=pl.CostEstimate(
            flops=4 * all_rows * 2 * keys * HD,
            bytes_accessed=2**22,
            transcendentals=all_rows * 2 * keys,
        ),
        name="attend",
    )(
        clip_order,
        key_counts,
        tile_mask,
        queries,
        noisy_keys,
        noisy_values,
        clean_keys,
        clean_values,
    )


def solution(mesh):
    split = P("section", ("ctx", "head"), None)
    return jax.shard_map(
        local,
        mesh=mesh,
        in_specs=(split,) * 5 + (P(),) * 3,
        out_specs=split,
        check_vma=False,
    )
```
